256 devices in a mesh: region: 64 (over z, x, core), batch: 4 (over y).
Axes of the slice: x: 4, y: 4, z: 8, core: 2. Of those that a mesh axis runs over, the one named last changes fastest.
Arguments:
- features: bfloat16 [64, 63, 32768], P('region', None, 'batch'), may hold values from -1 to 1
- spacing: float32 [64, 32768], P('region', 'batch'), may hold values from 6.8359375e-05 to 0.59375
- counts: int32 [64, 512], P('region', 'batch'), may hold values from 0 to 64, as said below
- depth_rank: int32 [512, 64], P('batch'), may hold values from 0 to 63, each once within a row
- target: float32 [3, 512], P(None, 'batch'), may hold values from 0 to 1
- w_in: float32 [64, 64, 256], P('region', 'batch'), may hold values from -0.75 to 0.75
- w_hid: float32 [64, 2, 256, 256], P('region', None, 'batch'), may hold values from -0.375 to 0.375
- b_hid: float32 [64, 2, 256], P('region', None, 'batch'), may hold values from -1.2 to 1.2
- w_out: float32 [64, 4, 256], P('region', None, 'batch'), may hold values from -0.375 to 0.375
- mom_in: float32 [2, 64, 64, 256], P(None, 'region', 'batch'), may hold values from -1 to 4, as said below
- mom_hid: float32 [2, 64, 2, 256, 256], P(None, 'region', None, 'batch'), may hold values from -1 to 4, as said below
- mom_bias: float32 [2, 64, 2, 256], P(None, 'region', None, 'batch'), may hold values from -1 to 4, as said below
- mom_out: float32 [2, 64, 4, 256], P(None, 'region', None, 'batch'), may hold values from -1 to 4, as said below
Outputs:
- new_w_in: float32 [64, 64, 256], P('region')
- new_w_hid: float32 [64, 2, 256, 256], P('region')
- new_b_hid: float32 [64, 2, 256], P('region')
- new_w_out: float32 [64, 4, 256], P('region')
- new_mom_in: float32 [2, 64, 64, 256], P(None, 'region', 'batch')
- new_mom_hid: float32 [2, 64, 2, 256, 256], P(None, 'region', None, 'batch')
- new_mom_bias: float32 [2, 64, 2, 256], P(None, 'region', None, 'batch')
- new_mom_out: float32 [2, 64, 4, 256], P(None, 'region', None, 'batch')
The draws below stay inside these ranges and needn't reach their ends.
Inputs may be any that keep to these rules, and one draw needn't show every extreme that they name: The first counts[c, ray] slots of a segment are live. `mom_in`: slice 0 is the first moment, slice 1 the second moment, which lies between 0.1 and 4. `mom_hid`: as for mom_in. `mom_bias`: as for mom_in. `mom_out`: as for mom_in.
All inputs are finite; a program needn't handle non-finite values.
Results may differ from the reference program's by a relative error of at most 0.012.
The reference program's roundings to bfloat16 on the way (of `act_one`, `act_two`, `act_three`, `grad_heads`, `back_three`, `back_two` and `back_one`) count: a program that leaves them out, or rounds other values in their place, can miss the bound.
Values may be sent and summed in bfloat16 or wider, within the bound.
No kernel may reach another device: no remote copies, remote signals or barrier semaphores. Data moves between devices by JAX's collectives and lax.ppermute only.
A program may use at most 128 MiB of HBM per device.

```python
import jax
import jax.numpy as jnp
from jax import lax

ENC = 63
HID = 256
S = 64
CELLS = 64
RAYS = 512


def draw_counts(key, part):
    key_top, key_choose, key_fill = jax.random.split(jax.random.fold_in(key, 5), 3)
    ceiling = jax.random.randint(key_top, (CELLS,), S // 8, S + 1)
    chosen = jax.random.permutation(key_choose, CELLS)
    ceiling = jnp.where(chosen == 0, S, ceiling)
    filled = jax.random.randint(key_fill, (CELLS, RAYS), 0, ceiling[:, None] + 1)
    filled = filled.at[:, 0].set(ceiling)
    return filled.astype(jnp.int32)


def draw_spacing(key, part):
    key_choose, key_levels, key_rough = jax.random.split(jax.random.fold_in(key, 7), 3)
    chooser = jax.random.uniform(key_choose, (CELLS, RAYS), jnp.float32)
    levels = jax.random.uniform(key_levels, (CELLS, RAYS), jnp.float32)
    rough_draw = jax.random.uniform(key_rough, (CELLS, RAYS, S), jnp.float32)
    lowest_depth = 2.0
    highest_depth = 10.0
    roughness = jnp.exp(jnp.log(0.5) + rough_draw * (jnp.log(2.0) - jnp.log(0.5)))
    dense_depth = jnp.exp(jnp.log(lowest_depth) + levels * (jnp.log(highest_depth) - jnp.log(lowest_depth)))
    thin_depth = jnp.exp(jnp.log(0.5) + levels * (jnp.log(4.0) - jnp.log(0.5))) / CELLS
    seg_depth = jnp.where(chooser < 2.0 / CELLS, dense_depth, thin_depth)
    intervals = seg_depth[:, :, None] * roughness / (0.7 * S)
    return intervals.reshape(CELLS, RAYS * S).astype(jnp.float32)


def moment_pair(key, shape):
    key_first, key_second = jax.random.split(key)
    first = jnp.clip(0.15 * jax.random.normal(key_first, shape, jnp.float32), -1.0, 1.0)
    second = jnp.exp(jax.random.uniform(key_second, shape, jnp.float32, jnp.log(0.25), jnp.log(4.0)))
    return jnp.stack([first, second])


def draw_mom_in(key, part):
    return moment_pair(jax.random.fold_in(key, 11), (CELLS, ENC + 1, HID))


def draw_mom_hid(key, part):
    return moment_pair(jax.random.fold_in(key, 12), (CELLS, 2, HID, HID))


def draw_mom_bias(key, part):
    return moment_pair(jax.random.fold_in(key, 13), (CELLS, 2, HID))


def draw_mom_out(key, part):
    return moment_pair(jax.random.fold_in(key, 14), (CELLS, 4, HID))


def steps_of(stream_key, dims, cuts, least, top_value):
    gain, own = 1.0, jax.random.fold_in(stream_key, 6)
    for axis_at, blocks in cuts:
        draws = jnp.exp(jax.random.uniform(jax.random.fold_in(own, axis_at), (blocks,), jnp.float32, least / len(cuts), top_value / len(cuts)))
        gain = gain * jnp.repeat(draws, dims[axis_at] // blocks).reshape([-1 if axis == axis_at else 1 for axis in range(len(dims))])
    return gain


def normal_values(key, extent, scale, limit, cuts=(), held_as=jnp.bfloat16):
    level = steps_of(key, extent, cuts, -0.22, 0.18) if cuts else 1.0
    entries = jax.random.normal(key, extent, jnp.float32) * scale * level
    return jnp.minimum(jnp.maximum(entries, -limit), limit).astype(held_as)


def setup_inputs(seed: int = 0) -> dict:
    arg_keys = jax.random.split(jax.random.key(seed), 14)
    features = jnp.clip(jax.random.uniform(arg_keys[0], (CELLS, ENC, RAYS * S), jnp.float32, -1.0, 1.0) * steps_of(arg_keys[0], (CELLS, ENC, RAYS * S), ((0, 64), (2, 4)), -0.4, 0.0), -1.0, 1.0).astype(jnp.bfloat16)
    spacing = draw_spacing(jax.random.fold_in(arg_keys[13], 71), 0)
    counts = draw_counts(jax.random.fold_in(arg_keys[13], 71), 0)
    depth_rank = jax.vmap(lambda own: jax.random.permutation(own, CELLS))(jax.random.split(arg_keys[3], RAYS)).reshape((RAYS, CELLS)).astype(jnp.int32)
    target = jnp.clip(1.0 * jax.random.uniform(arg_keys[4], (3, RAYS), jnp.float32) ** steps_of(arg_keys[4], (3, RAYS), ((1, 4),), -0.2, 0.2), 0.0, 1.0)
    w_in = normal_values(arg_keys[5], (CELLS, ENC + 1, HID), (ENC + 1) ** -0.5, 0.75, ((0, 64), (1, 4)), jnp.float32)
    w_hid = normal_values(arg_keys[6], (CELLS, 2, HID, HID), HID ** -0.5, 0.375, ((0, 64), (2, 4)), jnp.float32)
    b_hid = normal_values(arg_keys[7], (CELLS, 2, HID), 0.3, 1.2, ((0, 64), (2, 4)), jnp.float32)
    w_out = normal_values(arg_keys[8], (CELLS, 4, HID), HID ** -0.5, 0.375, ((0, 64), (2, 4)), jnp.float32)
    mom_in = draw_mom_in(jax.random.fold_in(arg_keys[13], 71), 0)
    mom_hid = draw_mom_hid(jax.random.fold_in(arg_keys[13], 71), 0)
    mom_bias = draw_mom_bias(jax.random.fold_in(arg_keys[13], 71), 0)
    mom_out = draw_mom_out(jax.random.fold_in(arg_keys[13], 71), 0)
    return {"features": features, "spacing": spacing, "counts": counts, "depth_rank": depth_rank, "target": target, "w_in": w_in, "w_hid": w_hid, "b_hid": b_hid, "w_out": w_out, "mom_in": mom_in, "mom_hid": mom_hid, "mom_bias": mom_bias, "mom_out": mom_out}


beta_first = 0.9
beta_second = 0.95
learn_rate = 0.01
norm_eps = 1e-06
adam_eps = 1e-08

def contract_first(left, right):
    return lax.dot_general(left, right, (((0,), (0,)), ((), ())), preferred_element_type=jnp.float32)

def contract_last(left, right):
    return lax.dot_general(left, right, (((1,), (1,)), ((), ())), preferred_element_type=jnp.float32)

def network(samples, wide_in, wide_hid, bias_hid, wide_out):
    enc_rows = samples.shape[0]
    pre_one = contract_first(wide_in[:enc_rows], samples) + wide_in[enc_rows][:, None].astype(jnp.float32)
    act_one = jnp.maximum(pre_one, 0.0).astype(jnp.bfloat16)
    pre_two = contract_first(wide_hid[0], act_one) + bias_hid[0][:, None]
    act_two = jnp.maximum(pre_two, 0.0).astype(jnp.bfloat16)
    pre_three = contract_first(wide_hid[1], act_two) + bias_hid[1][:, None]
    act_three = jnp.maximum(pre_three, 0.0).astype(jnp.bfloat16)
    heads = jnp.dot(wide_out, act_three, preferred_element_type=jnp.float32)
    return ((pre_one, act_one, pre_two, act_two, pre_three, act_three), heads)

def optical(heads, gaps, live_counts):
    rays = live_counts.shape[0]
    slot = lax.broadcasted_iota(jnp.int32, (rays, S), 1)
    live = (slot < live_counts[:, None]).astype(jnp.float32)
    density = jax.nn.softplus(heads[0]).reshape(rays, S)
    depth = density * gaps.reshape(rays, S) * live
    colours = jax.nn.sigmoid(heads[1:4])
    return (live, depth, colours)

def summarize(depth, colours):
    rays = depth.shape[0]
    cum_in = jnp.cumsum(depth, axis=1)
    weight = jnp.exp(-(cum_in - depth)) * -jnp.expm1(-depth)
    shade = colours.reshape(3, rays, S)
    seg_colour = lax.optimization_barrier(jnp.sum(weight[None] * shade, axis=2))
    log_trans = -cum_in[:, -1]
    return (seg_colour, log_trans, cum_in, weight)

def backward(samples, gaps, live, depth, cum_in, weight, colours, heads, acts, mats, grad_seg, grad_log):
    pre_one, act_one, pre_two, act_two, pre_three, act_three = acts
    wide_in, wide_hid, wide_out = mats
    rays = depth.shape[0]
    shade = colours.reshape(3, rays, S)
    emit = lax.optimization_barrier(jnp.sum(grad_seg[:, :, None] * shade, axis=0))
    carried = emit * weight
    after = lax.optimization_barrier(jnp.sum(carried, axis=1, keepdims=True)) - jnp.cumsum(carried, axis=1)
    grad_depth = emit * jnp.exp(-cum_in) - after - grad_log[:, None]
    grad_density = (grad_depth * live * gaps.reshape(rays, S)).reshape(1, -1) * jax.nn.sigmoid(heads[0:1])
    grad_shade = (grad_seg[:, :, None] * weight[None]).reshape(3, -1) * colours * (1.0 - colours)
    grad_heads = jnp.concatenate([grad_density, grad_shade], axis=0).astype(jnp.bfloat16)
    grad_out = contract_last(grad_heads, act_three)
    back_three = jnp.where(pre_three > 0, contract_first(wide_out, grad_heads), 0.0).astype(jnp.bfloat16)
    grad_third = contract_last(act_two, back_three)
    bias_third = lax.optimization_barrier(jnp.sum(back_three.astype(jnp.float32), axis=1))
    back_two = jnp.where(pre_two > 0, jnp.dot(wide_hid[1], back_three, preferred_element_type=jnp.float32), 0.0).astype(jnp.bfloat16)
    grad_second = contract_last(act_one, back_two)
    bias_second = lax.optimization_barrier(jnp.sum(back_two.astype(jnp.float32), axis=1))
    back_one = jnp.where(pre_one > 0, jnp.dot(wide_hid[0], back_two, preferred_element_type=jnp.float32), 0.0).astype(jnp.bfloat16)
    grad_first = contract_last(samples, back_one)
    bias_first = lax.optimization_barrier(jnp.sum(back_one.astype(jnp.float32), axis=1))
    grad_in = jnp.concatenate([grad_first, bias_first[None]], axis=0)
    grad_hid = jnp.stack([grad_second, grad_third])
    grad_bias = jnp.stack([bias_second, bias_third])
    return (grad_in, grad_hid, grad_bias, grad_out)

def adam_step(grad, param, moment, scale):
    scaled = grad * scale
    first = beta_first * moment[0] + (1.0 - beta_first) * scaled
    second = beta_second * moment[1] + (1.0 - beta_second) * scaled * scaled
    fresh = param - learn_rate * first / (jnp.sqrt(second) + adam_eps)
    return (fresh, jnp.stack([first, second]))

def reference(features, spacing, counts, depth_rank, target, w_in, w_hid, b_hid, w_out, mom_in, mom_hid, mom_bias, mom_out):
    param_count = (ENC + 1) * HID + 2 * HID * HID + 6 * HID

    def forward_cell(items):
        samples, gaps, live_counts, first_w, hid_w, hid_b, last_w = items
        acts, heads = network(samples, first_w.astype(jnp.bfloat16), hid_w.astype(jnp.bfloat16), hid_b, last_w.astype(jnp.bfloat16))
        live, depth, colours = optical(heads, gaps, live_counts)
        seg_colour, log_trans, cum_in, weight = summarize(depth, colours)
        return (seg_colour, log_trans)
    seg_colour, log_trans = lax.map(forward_cell, (features, spacing, counts, w_in, w_hid, b_hid, w_out))
    ranks = depth_rank.T
    earlier = ranks[None, :, :] < ranks[:, None, :]
    prefix = lax.optimization_barrier(jnp.sum(jnp.where(earlier, log_trans[None], 0.0), axis=1))
    reach = jnp.exp(prefix)
    lit = reach[:, None] * seg_colour
    colour = lax.optimization_barrier(jnp.sum(lit, axis=0))
    grad_colour = 2.0 * (colour - target)
    later = ranks[None, :, :] > ranks[:, None, :]
    behind = lax.optimization_barrier(jnp.sum(jnp.where(later[:, :, None, :], lit[None], 0.0), axis=1))
    grad_seg_all = reach[:, None] * grad_colour[None]
    grad_log_all = lax.optimization_barrier(jnp.sum(grad_colour[None] * behind, axis=1))

    def update_cell(items):
        samples, gaps, live_counts, first_w, hid_w, hid_b, last_w, grad_seg, grad_log, m_first, m_hid, m_bias, m_last = items
        mats = (first_w.astype(jnp.bfloat16), hid_w.astype(jnp.bfloat16), last_w.astype(jnp.bfloat16))
        acts, heads = network(samples, mats[0], mats[1], hid_b, mats[2])
        live, depth, colours = optical(heads, gaps, live_counts)
        seg_c, log_t, cum_in, weight = summarize(depth, colours)
        grads = backward(samples, gaps, live, depth, cum_in, weight, colours, heads, acts, mats, grad_seg, grad_log)
        total_sq = jnp.sum(grads[0] * grads[0]) + jnp.sum(grads[1] * grads[1]) + jnp.sum(grads[2] * grads[2]) + jnp.sum(grads[3] * grads[3])
        scale = lax.rsqrt(total_sq / param_count + norm_eps)
        new_in, mom_first = adam_step(grads[0], first_w, m_first, scale)
        new_hid, mom_second = adam_step(grads[1], hid_w, m_hid, scale)
        new_bias, mom_third = adam_step(grads[2], hid_b, m_bias, scale)
        new_out, mom_fourth = adam_step(grads[3], last_w, m_last, scale)
        return (new_in, new_hid, new_bias, new_out, mom_first, mom_second, mom_third, mom_fourth)
    results = lax.map(update_cell, (features, spacing, counts, w_in, w_hid, b_hid, w_out, grad_seg_all, grad_log_all, jnp.moveaxis(mom_in, 0, 1), jnp.moveaxis(mom_hid, 0, 1), jnp.moveaxis(mom_bias, 0, 1), jnp.moveaxis(mom_out, 0, 1)))
    return (results[0], results[1], results[2], results[3], jnp.moveaxis(results[4], 1, 0), jnp.moveaxis(results[5], 1, 0), jnp.moveaxis(results[6], 1, 0), jnp.moveaxis(results[7], 1, 0))
```

```python
import functools

import jax
import jax.numpy as jnp
from jax import lax
from jax.experimental import pallas as pl
from jax.experimental.pallas import tpu as pltpu
from jax.sharding import PartitionSpec as P

ENC = 63
HID = 256
S = 64
N_BATCH = 4
CHUNK = 1024
MIB = 1 << 20

beta_first = 0.9
beta_second = 0.95
learn_rate = 0.01
norm_eps = 1e-06
adam_eps = 1e-08

f32 = jnp.float32
bf16 = jnp.bfloat16

ROWS_IN = HID // 16
ROWS_HID = HID // N_BATCH
MISC = ROWS_IN + 2 * ROWS_HID
BLOCK = MISC + 16

VMEM_WHOLE = pl.BlockSpec(memory_space=pltpu.VMEM)
SMEM_WHOLE = pl.BlockSpec(memory_space=pltpu.SMEM)


def dot(left, right):
    return lax.dot_general(left, right, (((1,), (0,)), ((), ())), preferred_element_type=f32)


def dot_last(left, right):
    return lax.dot_general(left, right, (((1,), (1,)), ((), ())), preferred_element_type=f32)


def at_own_lanes(rows, own):
    source = lax.broadcasted_iota(jnp.int32, (ROWS_HID, HID), 0)
    lane = lax.broadcasted_iota(jnp.int32, (ROWS_HID, HID), 1)
    place = jnp.where(lane == source + own * ROWS_HID, 1.0, 0.0).astype(bf16)
    return dot(rows, place).astype(bf16)


def pack_weights(idx, w_in, w_hid, b_hid, w_out, out):
    out[0:ROWS_IN, :] = w_in[0].astype(bf16)
    for layer in range(2):
        at = ROWS_IN + layer * ROWS_HID
        out[at : at + ROWS_HID, :] = w_hid[0, layer].astype(bf16)
    bias = b_hid[0]
    top = bias.astype(bf16).astype(f32)
    middle = (bias - top).astype(bf16).astype(f32)
    rest = bias - top - middle
    rows = jnp.concatenate(
        [w_out[0], top, middle, rest, jnp.zeros((6, ROWS_HID), f32)], axis=0
    ).astype(bf16)
    out[MISC:BLOCK, :] = at_own_lanes(rows, idx[1])


def pack_state(idx, w_in, w_hid, w_out, mom_in, mom_hid, mom_bias, mom_out, out):
    def low(value):
        return (value - value.astype(bf16).astype(f32)).astype(bf16)

    out[0:ROWS_IN, :] = low(w_in[0])
    for layer in range(2):
        at = ROWS_IN + layer * ROWS_HID
        out[at : at + ROWS_HID, :] = low(w_hid[0, layer])
    rest = w_out[0] - w_out[0].astype(bf16).astype(f32)
    rows = jnp.concatenate([rest, jnp.zeros((12, ROWS_HID), f32)], axis=0)
    out[MISC:BLOCK, :] = at_own_lanes(rows.astype(bf16), idx[1])
    for moment in range(2):
        base = BLOCK * (moment + 1)
        out[base : base + ROWS_IN, :] = mom_in[moment, 0].astype(bf16)
        for layer in range(2):
            at = base + ROWS_IN + layer * ROWS_HID
            out[at : at + ROWS_HID, :] = mom_hid[moment, 0, layer].astype(bf16)
        rows = jnp.concatenate(
            [mom_out[moment, 0], mom_bias[moment, 0], jnp.zeros((10, ROWS_HID), f32)], axis=0
        )
        out[base + MISC : base + BLOCK, :] = at_own_lanes(rows.astype(bf16), idx[1])


def turn(rows):
    turned = jnp.concatenate([rows, rows], axis=0).T
    lane = lax.broadcasted_iota(jnp.int32, (S, 2 * S), 1)
    return jnp.where(lane < S, turned[:S], turned[S:])


def running_sum(values):
    row = lax.broadcasted_iota(jnp.int32, values.shape, 0)
    step = 1
    while step < S:
        values = values + jnp.where(row >= step, pltpu.roll(values, step, 0), 0.0)
        step *= 2
    return values


def one_minus_exp(depth):
    small = depth * (1.0 - depth * (0.5 - depth * (1.0 / 6.0 - depth * (1.0 / 24.0 - depth * (1.0 / 120.0)))))
    return jnp.where(depth < 0.1, small, 1.0 - jnp.exp(-depth))


def sigmoid(value):
    return 1.0 / (1.0 + jnp.exp(-value))


def forward_kernel(
    idx, own, from_one, from_two, from_three, feats, gaps, counts,
    act_one, act_two, act_three, wide_in, wide_hid, wide_misc, shading, summary,
    turned_in, turned_hid, bias_cols, out_rows, heads_rows,
):
    step = pl.program_id(0)
    tiles = CHUNK // 128

    @pl.when(step == 0)
    def _():
        misc = jnp.zeros((16, HID), f32)
        for back, block in enumerate((own, from_one, from_two, from_three)):
            owner = (idx[1] + N_BATCH - back) % N_BATCH
            wide_in[pl.ds(pl.multiple_of(owner * ROWS_IN, 16), ROWS_IN), :] = block[0:ROWS_IN, :]
            for layer in range(2):
                at = ROWS_IN + layer * ROWS_HID
                wide_hid[layer, pl.ds(pl.multiple_of(owner * ROWS_HID, 16), ROWS_HID), :] = block[
                    at : at + ROWS_HID, :
                ]
            misc = misc + block[MISC:BLOCK, :].astype(f32)
        wide_misc[...] = misc
        turned_in[...] = wide_in[...].astype(f32).T.astype(bf16)
        for layer in range(2):
            turned_hid[layer] = wide_hid[layer].astype(f32).T.astype(bf16)
        bias = misc[4:6] + misc[6:8] + misc[8:10]
        bias_cols[...] = jnp.concatenate([bias, jnp.zeros((6, HID), f32)], axis=0).T
        row = lax.broadcasted_iota(jnp.int32, (16, HID), 0)
        out_rows[...] = jnp.where(row < 4, misc, 0.0).astype(bf16)

    one = jnp.maximum(dot(turned_in[...], feats[...]), 0.0).astype(bf16)
    act_one[...] = one
    two = jnp.maximum(dot(turned_hid[0], one) + bias_cols[:, 0:1], 0.0).astype(bf16)
    act_two[...] = two
    three = jnp.maximum(dot(turned_hid[1], two) + bias_cols[:, 1:2], 0.0).astype(bf16)
    act_three[...] = three
    heads = dot(out_rows[...], three)
    for tile in range(tiles):
        at = pl.multiple_of((step * tiles + tile) * 8, 8)
        heads_rows[pl.ds(at, 8), :] = heads[0:8, tile * 128 : (tile + 1) * 128]

    @pl.when(step == pl.num_programs(0) - 1)
    def _():
        density = turn(heads_rows[pl.ds(0, S, stride=8), :])
        gap = turn(gaps[...])
        slot = lax.broadcasted_iota(jnp.int32, (S, 128), 0)
        live = jnp.where(slot < counts[...], 1.0, 0.0)
        soft = jnp.maximum(density, 0.0) + jnp.log1p(jnp.exp(-jnp.abs(density)))
        depth = soft * gap * live
        total = running_sum(depth)
        weight = jnp.exp(-(total - depth)) * one_minus_exp(depth)
        for channel in range(3):
            colour = sigmoid(turn(heads_rows[pl.ds(channel + 1, S, stride=8), :]))
            shading[channel] = colour
            summary[channel : channel + 1, :] = jnp.sum(weight * colour, axis=0, keepdims=True)
        summary[3:4, :] = -total[S - 1 : S]
        shading[3] = weight
        shading[4] = jnp.exp(-total)
        shading[5] = live * gap * sigmoid(density)


def composite(idx, table, ranks, target, shading, reach_rows, grad_rows):
    cells = ranks.shape[0]
    order = ranks[...]
    logs = table[pl.ds(3, cells, stride=4), :]
    prefix = jnp.zeros((cells, 128), f32)
    for cell in range(cells):
        prefix = prefix + jnp.where(
            ranks[cell : cell + 1, :] < order, table[4 * cell + 3 : 4 * cell + 4, :], 0.0
        )
    del logs
    reach = jnp.exp(prefix)
    reach_rows[...] = reach
    own_reach = reach_rows[pl.ds(idx[0], 1), :]
    later = order > ranks[pl.ds(idx[0], 1), :]
    grad_seg = []
    grad_log = jnp.zeros((1, 128), f32)
    for channel in range(3):
        lit = reach * table[pl.ds(channel, cells, stride=4), :]
        grad_colour = 2.0 * (jnp.sum(lit, axis=0, keepdims=True) - target[channel : channel + 1, :])
        behind = jnp.sum(jnp.where(later, lit, 0.0), axis=0, keepdims=True)
        grad_log = grad_log + grad_colour * behind
        grad_seg.append(own_reach * grad_colour)
    weight = shading[3]
    emit = grad_seg[0] * shading[0] + grad_seg[1] * shading[1] + grad_seg[2] * shading[2]
    carried = emit * weight
    running = running_sum(carried)
    after = running[S - 1 : S] - running
    grad_depth = emit * shading[4] - after - grad_log
    grad_rows[...] = jnp.zeros(grad_rows.shape, f32)
    grad_rows[pl.ds(0, S, stride=16), :] = turn(grad_depth * shading[5])
    for channel in range(3):
        colour = shading[channel]
        shade = grad_seg[channel] * weight * colour * (1.0 - colour)
        grad_rows[pl.ds(channel + 1, S, stride=16), :] = turn(shade)


def masked(act, back):
    return jnp.where(act > 0, back.astype(bf16), jnp.zeros((), bf16))


def first_row(rows):
    row = lax.broadcasted_iota(jnp.int32, rows.shape, 0)
    return jnp.where(row == 0, rows, 0.0)


def upper_kernel(
    idx, table, ranks, target, shading, wide_misc, act_two, act_three,
    back_three, grads,
    reach_rows, grad_rows, out_cols, sum_third, sum_out,
):
    step = pl.program_id(0)
    tiles = CHUNK // 128

    @pl.when(step == 0)
    def _():
        composite(idx, table, ranks, target, shading, reach_rows, grad_rows)
        row = lax.broadcasted_iota(jnp.int32, (16, HID), 0)
        out_cols[...] = jnp.where(row < 4, wide_misc[...], 0.0).T.astype(bf16)
        sum_third[...] = jnp.zeros(sum_third.shape, f32)
        sum_out[...] = jnp.zeros(sum_out.shape, f32)

    heads = jnp.concatenate(
        [
            grad_rows[pl.ds(pl.multiple_of((step * tiles + tile) * 16, 16), 16), :]
            for tile in range(tiles)
        ],
        axis=1,
    ).astype(bf16)
    three = act_three[...]
    back = masked(three, dot(out_cols[...], heads))
    back_three[...] = back
    sum_out[...] += dot_last(heads, three)
    ones = jnp.ones((16, CHUNK), bf16)
    sum_third[...] += dot_last(jnp.concatenate([act_two[...], ones], axis=0), back)

    @pl.when(step == pl.num_programs(0) - 1)
    def _():
        grads[0:HID, :] = sum_third[0:HID, :].astype(bf16)
        row = lax.broadcasted_iota(jnp.int32, (16, HID), 0)
        misc = jnp.where(row < 4, sum_out[...], jnp.where(row == 5, sum_third[HID : HID + 16, :], 0.0))
        grads[HID : HID + 16, :] = misc.astype(bf16)


def lower_kernel(
    wide_hid, feats, act_one, act_two, back_three,
    grads,
    sum_second, sum_first,
):
    step = pl.program_id(0)

    @pl.when(step == 0)
    def _():
        sum_second[...] = jnp.zeros(sum_second.shape, f32)
        sum_first[...] = jnp.zeros(sum_first.shape, f32)

    one = act_one[...]
    back_two = masked(act_two[...], dot(wide_hid[1], back_three[...]))
    ones = jnp.ones((16, CHUNK), bf16)
    sum_second[...] += dot_last(jnp.concatenate([one, ones], axis=0), back_two)
    back_one = masked(one, dot(wide_hid[0], back_two))
    sum_first[...] += dot_last(feats[...], back_one)

    @pl.when(step == pl.num_programs(0) - 1)
    def _():
        grads[0:HID, :] = sum_second[0:HID, :].astype(bf16)
        grads[HID : HID + 64, :] = sum_first[...].astype(bf16)
        row = lax.broadcasted_iota(jnp.int32, (16, HID), 0)
        misc = jnp.where(row == 4, sum_second[HID : HID + 16, :], 0.0)
        grads[HID + 64 : HID + 80, :] = misc.astype(bf16)


def adam(grad, first, second, scale):
    scaled = grad * scale
    first = beta_first * first + (1.0 - beta_first) * scaled
    second = beta_second * second + (1.0 - beta_second) * scaled * scaled
    return first, second, learn_rate * first / (jnp.sqrt(second) + adam_eps)


def update_kernel(
    idx,
    upper_0, upper_1, upper_2, upper_3,
    lower_0, lower_1, lower_2, lower_3,
    high_0, high_1, high_2, high_3,
    state_0, state_1, state_2, state_3,
    wide_misc, mom_in, mom_hid, mom_bias, mom_out,
    new_in, new_hid, new_bias, new_out,
    out_in, out_hid, out_bias, out_out,
    upper, lower,
):
    param_count = (ENC + 1) * HID + 2 * HID * HID + 6 * HID
    upper[...] = (upper_0[...].astype(f32) + upper_2[...].astype(f32)) + (
        upper_1[...].astype(f32) + upper_3[...].astype(f32)
    )
    lower[...] = (lower_0[...].astype(f32) + lower_2[...].astype(f32)) + (
        lower_1[...].astype(f32) + lower_3[...].astype(f32)
    )
    squares = jnp.sum(upper[...] * upper[...], axis=0, keepdims=True) + jnp.sum(
        lower[...] * lower[...], axis=0, keepdims=True
    )
    total = jnp.sum(squares, axis=1, keepdims=True)
    scale = lax.rsqrt(total / param_count + norm_eps)

    def fresh(grad, high, state, at, rows):
        _, _, change = adam(
            grad,
            state[BLOCK + at : BLOCK + at + rows, :].astype(f32),
            state[2 * BLOCK + at : 2 * BLOCK + at + rows, :].astype(f32),
            scale,
        )
        value = high[at : at + rows, :].astype(f32) + state[at : at + rows, :].astype(f32)
        return value - change

    highs = (high_0, high_1, high_2, high_3)
    states = (state_0, state_1, state_2, state_3)
    low_misc = jnp.zeros((16, HID), f32)
    first_misc = jnp.zeros((16, HID), f32)
    second_misc = jnp.zeros((16, HID), f32)
    for back in range(N_BATCH):
        owner = (idx[1] + N_BATCH - back) % N_BATCH
        high, state = highs[back], states[back]
        hid = pl.ds(pl.multiple_of(owner * ROWS_HID, 16), ROWS_HID)
        new_hid[0, 0, hid, :] = fresh(lower[hid, :], high, state, ROWS_IN, ROWS_HID)
        new_hid[0, 1, hid, :] = fresh(upper[hid, :], high, state, ROWS_IN + ROWS_HID, ROWS_HID)
        first = pl.ds(pl.multiple_of(owner * ROWS_IN, 16), ROWS_IN)
        grad = lower[pl.ds(pl.multiple_of(HID + owner * ROWS_IN, 16), ROWS_IN), :]
        new_in[0, first, :] = fresh(grad, high, state, 0, ROWS_IN)
        low_misc = low_misc + state[MISC:BLOCK, :].astype(f32)
        first_misc = first_misc + state[BLOCK + MISC : 2 * BLOCK, :].astype(f32)
        second_misc = second_misc + state[2 * BLOCK + MISC : 3 * BLOCK, :].astype(f32)

    grad_misc = upper[HID : HID + 16, :] + lower[HID + 64 : HID + 80, :]
    _, _, change = adam(grad_misc, first_misc, second_misc, scale)
    weights = wide_misc[...]
    new_out[0] = weights[0:4] + low_misc[0:4] - change[0:4]
    new_bias[0] = weights[4:6] + weights[6:8] + weights[8:10] - change[4:6]

    own = pl.ds(pl.multiple_of(idx[1] * ROWS_HID, 16), ROWS_HID)
    for layer, grads in ((0, lower), (1, upper)):
        moments = adam(grads[own, :], mom_hid[0, 0, layer], mom_hid[1, 0, layer], scale)
        out_hid[0, 0, layer] = moments[0]
        out_hid[1, 0, layer] = moments[1]
    grad = lower[pl.ds(pl.multiple_of(HID + idx[1] * ROWS_IN, 16), ROWS_IN), :]
    moments = adam(grad, mom_in[0, 0], mom_in[1, 0], scale)
    out_in[0, 0] = moments[0]
    out_in[1, 0] = moments[1]
    own_misc = jnp.zeros((16, ROWS_HID), f32)
    for owner in range(N_BATCH):
        part = grad_misc[:, owner * ROWS_HID : (owner + 1) * ROWS_HID]
        own_misc = own_misc + jnp.where(idx[1] == owner, part, 0.0)
    moments = adam(own_misc[0:4], mom_out[0, 0], mom_out[1, 0], scale)
    out_out[0, 0] = moments[0]
    out_out[1, 0] = moments[1]
    moments = adam(own_misc[4:6], mom_bias[0, 0], mom_bias[1, 0], scale)
    out_bias[0, 0] = moments[0]
    out_bias[1, 0] = moments[1]


def params(limit=48):
    return pltpu.CompilerParams(vmem_limit_bytes=limit * MIB)


def from_others(block):
    return [
        lax.ppermute(block, "batch", [(i, (i + hop) % N_BATCH) for i in range(N_BATCH)])
        for hop in (1, 2, 3)
    ]


def shape(dims, dtype=f32):
    return jax.ShapeDtypeStruct(dims, dtype)


def body(
    inner,
    features, spacing, counts, depth_rank, target,
    w_in, w_hid, b_hid, w_out,
    mom_in, mom_hid, mom_bias, mom_out,
):
    samples = features.shape[2]
    rays = samples // S
    cells = depth_rank.shape[1]
    steps = samples // CHUNK
    outer = cells // inner
    idx = jnp.stack([lax.axis_index("region"), lax.axis_index("batch")]).astype(jnp.int32)

    block = pl.pallas_call(
        pack_weights,
        out_shape=shape((BLOCK, HID), bf16),
        in_specs=[SMEM_WHOLE] + [VMEM_WHOLE] * 4,
        out_specs=VMEM_WHOLE,
        name="pack_weights",
    )(idx, w_in, w_hid, b_hid, w_out)
    highs = [block] + from_others(block)
    state = pl.pallas_call(
        pack_state,
        out_shape=shape((3 * BLOCK, HID), bf16),
        in_specs=[SMEM_WHOLE] + [VMEM_WHOLE] * 7,
        out_specs=VMEM_WHOLE,
        name="pack_state",
    )(idx, w_in, w_hid, w_out, mom_in, mom_hid, mom_bias, mom_out)
    states = [state] + from_others(state)

    feats = jnp.concatenate([features[0], jnp.ones((1, samples), bf16)], axis=0)
    gaps = spacing[0].reshape(rays // 2, 2 * S)
    live_counts = counts[0].reshape(rays // 2, 2).T.reshape(1, rays)
    ranks = depth_rank.reshape(rays // 2, 2, cells).transpose(2, 1, 0).reshape(cells, rays)
    goal = target.reshape(3, rays // 2, 2).transpose(0, 2, 1).reshape(3, rays)

    columns = lambda rows: pl.BlockSpec((rows, CHUNK), lambda i: (0, i))
    whole = lambda *dims: pl.BlockSpec(dims, lambda i: (0,) * len(dims))
    act = shape((HID, samples), bf16)
    act_one, act_two, act_three, wide_in, wide_hid, wide_misc, shading, summary = pl.pallas_call(
        forward_kernel,
        grid=(steps,),
        out_shape=(
            act, act, act, shape((ENC + 1, HID), bf16), shape((2, HID, HID), bf16),
            shape((16, HID)), shape((6, S, 128)), shape((4, rays)),
        ),
        in_specs=[SMEM_WHOLE] + [whole(BLOCK, HID)] * 4
        + [columns(ENC + 1), whole(rays // 2, 2 * S), whole(1, rays)],
        out_specs=(
            columns(HID), columns(HID), columns(HID), whole(ENC + 1, HID), whole(2, HID, HID),
            whole(16, HID), whole(6, S, 128), whole(4, rays),
        ),
        scratch_shapes=[
            pltpu.VMEM((HID, ENC + 1), bf16),
            pltpu.VMEM((2, HID, HID), bf16),
            pltpu.VMEM((HID, 8), f32),
            pltpu.VMEM((16, HID), bf16),
            pltpu.VMEM((samples // 16, 128), f32),
        ],
        compiler_params=params(),
        name="forward",
    )(idx, *highs, feats, gaps, live_counts)

    near = [[z * inner + i for i in range(inner)] for z in range(outer)]
    far = [[z * inner + i for z in range(outer)] for i in range(inner)]
    some = lax.all_to_all(
        jnp.broadcast_to(summary[None], (inner, 4, rays)), "region", 0, 0,
        axis_index_groups=near, tiled=True,
    )
    table = lax.all_to_all(
        jnp.broadcast_to(some[None], (outer, inner, 4, rays)), "region", 0, 0,
        axis_index_groups=far, tiled=True,
    ).reshape(cells * 4, rays)

    back_three, grads_upper = pl.pallas_call(
        upper_kernel,
        grid=(steps,),
        out_shape=(act, shape((HID + 16, HID), bf16)),
        in_specs=[
            SMEM_WHOLE, whole(cells * 4, rays), whole(cells, rays), whole(3, rays),
            whole(6, S, 128), whole(16, HID), columns(HID), columns(HID),
        ],
        out_specs=(columns(HID), whole(HID + 16, HID)),
        scratch_shapes=[
            pltpu.VMEM((cells, 128), f32),
            pltpu.VMEM((samples // 8, 128), f32),
            pltpu.VMEM((HID, 16), bf16),
            pltpu.VMEM((HID + 16, HID), f32),
            pltpu.VMEM((16, HID), f32),
        ],
        compiler_params=params(),
        name="upper",
    )(idx, table, ranks, goal, shading, wide_misc, act_two, act_three)
    uppers = [grads_upper] + from_others(grads_upper)

    grads_lower = pl.pallas_call(
        lower_kernel,
        grid=(steps,),
        out_shape=shape((HID + 80, HID), bf16),
        in_specs=[
            whole(2, HID, HID), columns(ENC + 1), columns(HID), columns(HID), columns(HID),
        ],
        out_specs=whole(HID + 80, HID),
        scratch_shapes=[
            pltpu.VMEM((HID + 16, HID), f32),
            pltpu.VMEM((64, HID), f32),
        ],
        compiler_params=params(),
        cost_estimate=pl.CostEstimate(
            flops=7 * samples * HID * HID, bytes_accessed=26 * samples * HID // 4, transcendentals=0
        ),
        name="lower",
    )(wide_hid, feats, act_one, act_two, back_three)
    lowers = [grads_lower] + from_others(grads_lower)

    return pl.pallas_call(
        update_kernel,
        out_shape=(
            shape((1, ENC + 1, HID)), shape((1, 2, HID, HID)), shape((1, 2, HID)), shape((1, 4, HID)),
            shape(mom_in.shape), shape(mom_hid.shape), shape(mom_bias.shape), shape(mom_out.shape),
        ),
        in_specs=[SMEM_WHOLE] + [VMEM_WHOLE] * 21,
        out_specs=(VMEM_WHOLE,) * 8,
        scratch_shapes=[
            pltpu.VMEM((HID + 16, HID), f32),
            pltpu.VMEM((HID + 80, HID), f32),
        ],
        compiler_params=params(),
        name="update",
    )(idx, *uppers, *lowers, *highs, *states, wide_misc, mom_in, mom_hid, mom_bias, mom_out)


def solution(mesh):
    cells = mesh.shape["region"]
    inner = 8 if cells % 8 == 0 and cells > 8 else 2
    return jax.shard_map(
        functools.partial(body, inner),
        mesh=mesh,
        in_specs=(
            P("region", None, "batch"),
            P("region", "batch"),
            P("region", "batch"),
            P("batch", None),
            P(None, "batch"),
            P("region", "batch", None),
            P("region", None, "batch", None),
            P("region", None, "batch"),
            P("region", None, "batch"),
            P(None, "region", "batch", None),
            P(None, "region", None, "batch", None),
            P(None, "region", None, "batch"),
            P(None, "region", None, "batch"),
        ),
        out_specs=(
            P("region", None, None),
            P("region", None, None, None),
            P("region", None, None),
            P("region", None, None),
            P(None, "region", "batch", None),
            P(None, "region", None, "batch", None),
            P(None, "region", None, "batch"),
            P(None, "region", None, "batch"),
        ),
        check_vma=False,
    )
```

```python
import functools

import jax
import jax.numpy as jnp
from jax import lax
from jax.experimental import pallas as pl
from jax.experimental.pallas import tpu as pltpu
from jax.sharding import PartitionSpec as P

ENC = 63
HID = 256
S = 64
N_BATCH = 4
CHUNK = 4096
MIB = 1 << 20
LIMIT = 24

beta_first = 0.9
beta_second = 0.95
learn_rate = 0.01
norm_eps = 1e-06
adam_eps = 1e-08

f32 = jnp.float32
bf16 = jnp.bfloat16

ROWS_IN = HID // 16
ROWS_HID = HID // N_BATCH
MISC = ROWS_IN + 2 * ROWS_HID
BLOCK = MISC + 16


def dot(left, right):
    return lax.dot_general(left, right, (((1,), (0,)), ((), ())), preferred_element_type=f32)


def dot_last(left, right):
    return lax.dot_general(left, right, (((1,), (1,)), ((), ())), preferred_element_type=f32)


def at_own_lanes(rows, own):
    source = lax.broadcasted_iota(jnp.int32, (ROWS_HID, HID), 0)
    lane = lax.broadcasted_iota(jnp.int32, (ROWS_HID, HID), 1)
    place = jnp.where(lane == source + own * ROWS_HID, 1.0, 0.0).astype(bf16)
    return dot(rows, place).astype(bf16)


def pack_weights(w_in, w_hid, b_hid, w_out, out):
    out[0:ROWS_IN, :] = w_in[0].astype(bf16)
    for layer in range(2):
        at = ROWS_IN + layer * ROWS_HID
        out[at : at + ROWS_HID, :] = w_hid[0, layer].astype(bf16)
    bias = b_hid[0]
    top = bias.astype(bf16).astype(f32)
    middle = (bias - top).astype(bf16).astype(f32)
    rest = bias - top - middle
    rows = jnp.concatenate(
        [w_out[0], top, middle, rest, jnp.zeros((6, ROWS_HID), f32)], axis=0
    ).astype(bf16)
    out[MISC:BLOCK, :] = at_own_lanes(rows, lax.axis_index("batch"))


def by_lane(rows):
    ray = lax.broadcasted_iota(jnp.int32, (128, 128), 0)
    lane = lax.broadcasted_iota(jnp.int32, (128, 128), 1)
    place = jnp.where(ray == jnp.where(lane < S, 2 * lane, 2 * (lane - S) + 1), 1.0, 0.0)
    return dot(rows.astype(bf16), place.astype(bf16))


def prepare_kernel(
    w_in, w_hid, w_out, mom_in, mom_hid, mom_bias, mom_out, spacing, counts, ranks, target,
    out, gaps, live_counts, order, goal,
):
    own = lax.axis_index("batch")

    def low(value):
        return (value - value.astype(bf16).astype(f32)).astype(bf16)

    out[0:ROWS_IN, :] = low(w_in[0])
    for layer in range(2):
        at = ROWS_IN + layer * ROWS_HID
        out[at : at + ROWS_HID, :] = low(w_hid[0, layer])
    rest = w_out[0] - w_out[0].astype(bf16).astype(f32)
    rows = jnp.concatenate([rest, jnp.zeros((12, ROWS_HID), f32)], axis=0)
    out[MISC:BLOCK, :] = at_own_lanes(rows.astype(bf16), own)
    for moment in range(2):
        base = BLOCK * (moment + 1)
        out[base : base + ROWS_IN, :] = mom_in[moment, 0].astype(bf16)
        for layer in range(2):
            at = base + ROWS_IN + layer * ROWS_HID
            out[at : at + ROWS_HID, :] = mom_hid[moment, 0, layer].astype(bf16)
        rows = jnp.concatenate(
            [mom_out[moment, 0], mom_bias[moment, 0], jnp.zeros((10, ROWS_HID), f32)], axis=0
        )
        out[base + MISC : base + BLOCK, :] = at_own_lanes(rows.astype(bf16), own)

    gaps[...] = turn(spacing[...])
    order[...] = by_lane(ranks[...].astype(f32))
    top = target[...].astype(bf16).astype(f32)
    middle = (target[...] - top).astype(bf16).astype(f32)
    rest = target[...] - top - middle
    number = counts[...].astype(f32)
    moved = by_lane(jnp.concatenate([top, middle, rest, number, jnp.zeros((6, 128), f32)], axis=0))
    goal[...] = moved[0:3] + moved[3:6] + moved[6:9]
    live_counts[...] = moved[9:10]


def turn(rows):
    turned = jnp.concatenate([rows, rows], axis=0).T
    lane = lax.broadcasted_iota(jnp.int32, (S, 2 * S), 1)
    return jnp.where(lane < S, turned[:S], turned[S:])


def running_sum(values):
    row = lax.broadcasted_iota(jnp.int32, values.shape, 0)
    step = 1
    while step < S:
        values = values + jnp.where(row >= step, pltpu.roll(values, step, 0), 0.0)
        step *= 2
    return values


def one_minus_exp(depth):
    small = depth * (1.0 - depth * (0.5 - depth * (1.0 / 6.0 - depth * (1.0 / 24.0 - depth * (1.0 / 120.0)))))
    return jnp.where(depth < 0.1, small, 1.0 - jnp.exp(-depth))


def rectified(value):
    return jnp.maximum(value.astype(bf16), jnp.zeros((), bf16))


def sigmoid(value):
    return 1.0 / (1.0 + jnp.exp(-value))


def forward_kernel(
    own, from_one, from_two, from_three, feats, gaps, counts,
    act_one, act_two, act_three, wide_hid, wide_misc, shading, summary,
    wide_in, turned_in, turned_hid, bias_cols, out_rows, heads_rows,
):
    me = lax.axis_index("batch")
    misc = jnp.zeros((16, HID), f32)
    for back, block in enumerate((own, from_one, from_two, from_three)):
        owner = lax.rem(me + N_BATCH - back, N_BATCH)
        wide_in[pl.ds(pl.multiple_of(owner * ROWS_IN, 16), ROWS_IN), :] = block[0:ROWS_IN, :]
        for layer in range(2):
            at = ROWS_IN + layer * ROWS_HID
            wide_hid[layer, pl.ds(pl.multiple_of(owner * ROWS_HID, 16), ROWS_HID), :] = block[
                at : at + ROWS_HID, :
            ]
        misc = misc + block[MISC:BLOCK, :].astype(f32)
    wide_misc[...] = misc
    turned_in[...] = wide_in[...].astype(f32).T.astype(bf16)
    for layer in range(2):
        turned_hid[layer] = wide_hid[layer].astype(f32).T.astype(bf16)
    bias = misc[4:6] + misc[6:8] + misc[8:10]
    bias_cols[...] = jnp.concatenate([bias, jnp.zeros((6, HID), f32)], axis=0).T
    row = lax.broadcasted_iota(jnp.int32, (16, HID), 0)
    out_rows[...] = jnp.where(row < 4, misc, 0.0).astype(bf16)

    @pl.loop(0, feats.shape[1] // CHUNK)
    def _(step):
        columns = pl.ds(pl.multiple_of(step * CHUNK, CHUNK), CHUNK)
        one = rectified(dot(turned_in[...], feats[:, columns]))
        act_one[:, columns] = one
        two = rectified(dot(turned_hid[0], one) + bias_cols[:, 0:1])
        act_two[:, columns] = two
        three = rectified(dot(turned_hid[1], two) + bias_cols[:, 1:2])
        act_three[:, columns] = three
        heads = dot(out_rows[...], three)
        for tile in range(CHUNK // 128):
            at = pl.multiple_of((step * (CHUNK // 128) + tile) * 8, 8)
            heads_rows[pl.ds(at, 8), :] = heads[0:8, tile * 128 : (tile + 1) * 128]

    density = turn(heads_rows[pl.ds(0, S, stride=8), :])
    slot = lax.broadcasted_iota(jnp.int32, (S, 128), 0).astype(f32)
    live_gap = jnp.where(slot < counts[...], gaps[...], 0.0)
    soft = jnp.maximum(density, 0.0) + jnp.log1p(jnp.exp(-jnp.abs(density)))
    depth = soft * live_gap
    total = running_sum(depth)
    weight = jnp.exp(-(total - depth)) * one_minus_exp(depth)
    for channel in range(3):
        colour = sigmoid(turn(heads_rows[pl.ds(channel + 1, S, stride=8), :]))
        shading[channel] = colour
        summary[channel : channel + 1, :] = jnp.sum(weight * colour, axis=0, keepdims=True)
    summary[3:4, :] = -total[S - 1 : S]
    shading[3] = weight
    shading[4] = jnp.exp(-total)
    shading[5] = live_gap * sigmoid(density)


def composite(table, ranks, target, shading, reach_rows, grad_rows):
    cells = ranks.shape[0]
    order = ranks[...]
    own = lax.axis_index("region")
    prefix = jnp.zeros((cells, 128), f32)
    for cell in range(cells):
        prefix = prefix + jnp.where(
            ranks[cell : cell + 1, :] < order, table[4 * cell + 3 : 4 * cell + 4, :], 0.0
        )
    reach = jnp.exp(prefix)
    reach_rows[...] = reach
    own_reach = reach_rows[pl.ds(own, 1), :]
    later = order > ranks[pl.ds(own, 1), :]
    grad_seg = []
    grad_log = jnp.zeros((1, 128), f32)
    for channel in range(3):
        lit = reach * table[pl.ds(channel, cells, stride=4), :]
        grad_colour = 2.0 * (jnp.sum(lit, axis=0, keepdims=True) - target[channel : channel + 1, :])
        behind = jnp.sum(jnp.where(later, lit, 0.0), axis=0, keepdims=True)
        grad_log = grad_log + grad_colour * behind
        grad_seg.append(own_reach * grad_colour)
    weight = shading[3]
    emit = grad_seg[0] * shading[0] + grad_seg[1] * shading[1] + grad_seg[2] * shading[2]
    carried = emit * weight
    running = running_sum(carried)
    after = running[S - 1 : S] - running
    grad_depth = emit * shading[4] - after - grad_log
    grad_rows[...] = jnp.zeros(grad_rows.shape, f32)
    grad_rows[pl.ds(0, S, stride=16), :] = turn(grad_depth * shading[5])
    for channel in range(3):
        colour = shading[channel]
        shade = grad_seg[channel] * weight * colour * (1.0 - colour)
        grad_rows[pl.ds(channel + 1, S, stride=16), :] = turn(shade)


def masked(act, back):
    return jnp.where(act > 0, back.astype(bf16), jnp.zeros((), bf16))


def backward_kernel(
    table, ranks, target, shading, wide_hid, wide_misc, feats, act_one, act_two, act_three,
    even, odd,
    reach_rows, grad_rows, out_cols, sum_third, sum_second, sum_first, sum_out,
):
    composite(table, ranks, target, shading, reach_rows, grad_rows)
    row = lax.broadcasted_iota(jnp.int32, (16, HID), 0)
    out_cols[...] = jnp.where(row < 4, wide_misc[...], 0.0).T.astype(bf16)
    for total in (sum_third, sum_second, sum_first, sum_out):
        total[...] = jnp.zeros(total.shape, f32)

    @pl.loop(0, feats.shape[1] // CHUNK)
    def _(step):
        columns = pl.ds(pl.multiple_of(step * CHUNK, CHUNK), CHUNK)
        tiles = CHUNK // 128
        heads = jnp.concatenate(
            [
                grad_rows[pl.ds(pl.multiple_of((step * tiles + tile) * 16, 16), 16), :]
                for tile in range(tiles)
            ],
            axis=1,
        ).astype(bf16)
        ones = jnp.ones((16, CHUNK), bf16)
        one, two, three = act_one[:, columns], act_two[:, columns], act_three[:, columns]
        back_three = masked(three, dot(out_cols[...], heads))
        sum_out[...] += dot_last(heads, three)
        back_two = masked(two, dot(wide_hid[1], back_three))
        sum_third[...] += dot_last(jnp.concatenate([two, ones], axis=0), back_three)
        back_one = masked(one, dot(wide_hid[0], back_two))
        sum_second[...] += dot_last(jnp.concatenate([one, ones], axis=0), back_two)
        sum_first[...] += dot_last(feats[:, columns], back_one)

    misc = jnp.where(row < 4, sum_out[...], 0.0)
    misc = misc + jnp.where(row == 4, sum_second[HID : HID + 16, :], 0.0)
    misc = misc + jnp.where(row == 5, sum_third[HID : HID + 16, :], 0.0)
    even[0:HID, :] = sum_third[0:HID, :].astype(bf16)
    even[HID : HID + 32, :] = sum_first[0:32, :].astype(bf16)
    even[HID + 32 : HID + 48, :] = misc.astype(bf16)
    odd[0:HID, :] = sum_second[0:HID, :].astype(bf16)
    odd[HID : HID + 32, :] = sum_first[32:64, :].astype(bf16)


def pair_kernel(even, even_other, odd, odd_other, even_sum, odd_sum):
    even_sum[...] = (even[...].astype(f32) + even_other[...].astype(f32)).astype(bf16)
    odd_sum[...] = (odd[...].astype(f32) + odd_other[...].astype(f32)).astype(bf16)


def adam(grad, first, second, scale):
    scaled = grad * scale
    first = beta_first * first + (1.0 - beta_first) * scaled
    second = beta_second * second + (1.0 - beta_second) * scaled * scaled
    return first, second, learn_rate * first / (jnp.sqrt(second) + adam_eps)


def update_kernel(
    even, even_other, odd, odd_other,
    high_0, high_1, high_2, high_3,
    state_0, state_1, state_2, state_3,
    wide_misc, mom_in, mom_hid, mom_bias, mom_out,
    new_in, new_hid, new_bias, new_out,
    out_in, out_hid, out_bias, out_out,
    upper, lower, first_rows,
):
    me = lax.axis_index("batch")
    param_count = (ENC + 1) * HID + 2 * HID * HID + 6 * HID
    upper[...] = even[...].astype(f32) + even_other[...].astype(f32)
    lower[...] = odd[...].astype(f32) + odd_other[...].astype(f32)
    first_rows[0:32, :] = upper[HID : HID + 32, :]
    first_rows[32:64, :] = lower[HID : HID + 32, :]
    grad_misc = upper[HID + 32 : HID + 48, :]
    squares = jnp.sum(upper[...] * upper[...], axis=0, keepdims=True) + jnp.sum(
        lower[...] * lower[...], axis=0, keepdims=True
    )
    total = jnp.sum(squares, axis=1, keepdims=True)
    scale = lax.rsqrt(total / param_count + norm_eps)

    def fresh(grad, high, state, at, rows):
        _, _, change = adam(
            grad,
            state[BLOCK + at : BLOCK + at + rows, :].astype(f32),
            state[2 * BLOCK + at : 2 * BLOCK + at + rows, :].astype(f32),
            scale,
        )
        value = high[at : at + rows, :].astype(f32) + state[at : at + rows, :].astype(f32)
        return value - change

    highs = (high_0, high_1, high_2, high_3)
    states = (state_0, state_1, state_2, state_3)
    low_misc = jnp.zeros((16, HID), f32)
    first_misc = jnp.zeros((16, HID), f32)
    second_misc = jnp.zeros((16, HID), f32)
    for back in range(N_BATCH):
        owner = lax.rem(me + N_BATCH - back, N_BATCH)
        high, state = highs[back], states[back]
        hid = pl.ds(pl.multiple_of(owner * ROWS_HID, 16), ROWS_HID)
        new_hid[0, 0, hid, :] = fresh(lower[hid, :], high, state, ROWS_IN, ROWS_HID)
        new_hid[0, 1, hid, :] = fresh(upper[hid, :], high, state, ROWS_IN + ROWS_HID, ROWS_HID)
        first = pl.ds(pl.multiple_of(owner * ROWS_IN, 16), ROWS_IN)
        grad = first_rows[first, :]
        new_in[0, first, :] = fresh(grad, high, state, 0, ROWS_IN)
        low_misc = low_misc + state[MISC:BLOCK, :].astype(f32)
        first_misc = first_misc + state[BLOCK + MISC : 2 * BLOCK, :].astype(f32)
        second_misc = second_misc + state[2 * BLOCK + MISC : 3 * BLOCK, :].astype(f32)

    _, _, change = adam(grad_misc, first_misc, second_misc, scale)
    weights = wide_misc[...]
    new_out[0] = weights[0:4] + low_misc[0:4] - change[0:4]
    new_bias[0] = weights[4:6] + weights[6:8] + weights[8:10] - change[4:6]

    own = pl.ds(pl.multiple_of(me * ROWS_HID, 16), ROWS_HID)
    for layer, grads in ((0, lower), (1, upper)):
        moments = adam(grads[own, :], mom_hid[0, 0, layer], mom_hid[1, 0, layer], scale)
        out_hid[0, 0, layer] = moments[0]
        out_hid[1, 0, layer] = moments[1]
    grad = first_rows[pl.ds(pl.multiple_of(me * ROWS_IN, 16), ROWS_IN), :]
    moments = adam(grad, mom_in[0, 0], mom_in[1, 0], scale)
    out_in[0, 0] = moments[0]
    out_in[1, 0] = moments[1]
    own_misc = jnp.zeros((16, ROWS_HID), f32)
    for owner in range(N_BATCH):
        part = grad_misc[:, owner * ROWS_HID : (owner + 1) * ROWS_HID]
        own_misc = own_misc + jnp.where(me == owner, part, 0.0)
    moments = adam(own_misc[0:4], mom_out[0, 0], mom_out[1, 0], scale)
    out_out[0, 0] = moments[0]
    out_out[1, 0] = moments[1]
    moments = adam(own_misc[4:6], mom_bias[0, 0], mom_bias[1, 0], scale)
    out_bias[0, 0] = moments[0]
    out_bias[1, 0] = moments[1]


def fetched(kernel, fetch, outs):
    def run(*refs):
        sources, rest = refs[:fetch], refs[fetch : fetch + outs]
        copies, sem = refs[fetch + outs : -1], refs[-1]
        moves = [pltpu.make_async_copy(a, b, sem.at[i]) for i, (a, b) in enumerate(zip(sources, copies))]
        for move in moves:
            move.start()
        for move in moves:
            move.wait()
        kernel(*copies, *rest)

    return run


def call_on_hbm(kernel, outs, name, *arrays):
    outs = outs if isinstance(outs, tuple) else (outs,)
    return pl.pallas_call(
        fetched(kernel, len(arrays), len(outs)),
        out_shape=outs,
        in_specs=[pl.BlockSpec(memory_space=pltpu.HBM)] * len(arrays),
        scratch_shapes=[pltpu.VMEM(a.shape, a.dtype) for a in arrays]
        + [pltpu.SemaphoreType.DMA((len(arrays),))],
        compiler_params=pltpu.CompilerParams(vmem_limit_bytes=60 * MIB),
        name=name,
    )(*arrays)


def call(kernel, outs, scratch=(), name=None):
    return pl.pallas_call(
        kernel,
        out_shape=outs,
        scratch_shapes=[pltpu.VMEM(*s) for s in scratch],
        compiler_params=pltpu.CompilerParams(vmem_limit_bytes=LIMIT * MIB),
        name=name,
    )


def from_others(block):
    return [
        lax.ppermute(block, "batch", [(i, (i + hop) % N_BATCH) for i in range(N_BATCH)])
        for hop in (1, 2, 3)
    ]


def swapped(block, first):
    pairs = [(0, 1), (2, 3)] if first else [(1, 2), (3, 0)]
    return lax.ppermute(block, "batch", pairs + [(j, i) for i, j in pairs])


def held(dims, dtype=f32):
    return pltpu.VMEM(dims, dtype)


def shape(dims, dtype=f32):
    return jax.ShapeDtypeStruct(dims, dtype)


def body(
    inner,
    features, spacing, counts, depth_rank, target,
    w_in, w_hid, b_hid, w_out,
    mom_in, mom_hid, mom_bias, mom_out,
):
    samples = features.shape[2]
    rays = samples // S
    cells = depth_rank.shape[1]
    outer = cells // inner

    (block,) = call_on_hbm(
        pack_weights, held((BLOCK, HID), bf16), "pack_weights", w_in, w_hid, b_hid, w_out
    )
    block, spacing = lax.optimization_barrier((block, spacing))
    highs = [block] + from_others(block)
    state, gaps, live_counts, ranks, goal = call_on_hbm(
        prepare_kernel,
        (
            held((3 * BLOCK, HID), bf16), held((S, rays)), held((1, rays)), held((cells, rays)),
            held((3, rays)),
        ),
        "prepare",
        w_in, w_hid, w_out, mom_in, mom_hid, mom_bias, mom_out,
        spacing.reshape(rays // 2, 2 * S), counts, depth_rank.T, target,
    )
    state, highs[1] = lax.optimization_barrier((state, highs[1]))
    states = [state] + from_others(state)
    feats = jnp.concatenate([features[0], jnp.ones((1, samples), bf16)], axis=0)

    act = held((HID, samples), bf16)
    act_one, act_two, act_three, wide_hid, wide_misc, shading, summary = call(
        forward_kernel,
        (
            act, act, act, held((2, HID, HID), bf16),
            held((16, HID)), held((6, S, 128)), held((4, rays)),
        ),
        scratch=[
            ((ENC + 1, HID), bf16), ((HID, ENC + 1), bf16), ((2, HID, HID), bf16), ((HID, 8), f32),
            ((16, HID), bf16), ((samples // 16, 128), f32),
        ],
        name="forward",
    )(*highs, feats, gaps, live_counts)

    summary, *states = lax.optimization_barrier((summary, *states))
    near = [[z * inner + i for i in range(inner)] for z in range(outer)]
    far = [[z * inner + i for z in range(outer)] for i in range(inner)]
    some = lax.all_to_all(
        jnp.broadcast_to(summary[None], (inner, 4, rays)), "region", 0, 0,
        axis_index_groups=near, tiled=True,
    )
    table = lax.all_to_all(
        jnp.broadcast_to(some[None], (outer, inner, 4, rays)), "region", 0, 0,
        axis_index_groups=far, tiled=True,
    ).reshape(cells * 4, rays)

    even, odd = call(
        backward_kernel,
        (held((HID + 48, HID), bf16), held((HID + 32, HID), bf16)),
        scratch=[
            ((cells, 128), f32), ((samples // 8, 128), f32), ((HID, 16), bf16), ((HID + 16, HID), f32),
            ((HID + 16, HID), f32), ((64, HID), f32), ((16, HID), f32),
        ],
        name="backward",
    )(table, ranks, goal, shading, wide_hid, wide_misc, feats, act_one, act_two, act_three)
    even, odd = call(
        pair_kernel, (held(even.shape, bf16), held(odd.shape, bf16)), name="pair"
    )(even, swapped(even, True), odd, swapped(odd, False))

    return call(
        update_kernel,
        (
            shape((1, ENC + 1, HID)), shape((1, 2, HID, HID)), shape((1, 2, HID)), shape((1, 4, HID)),
            shape(mom_in.shape), shape(mom_hid.shape), shape(mom_bias.shape), shape(mom_out.shape),
        ),
        scratch=[((HID + 48, HID), f32), ((HID + 32, HID), f32), ((64, HID), f32)],
        name="update",
    )(
        even, swapped(even, False), odd, swapped(odd, True),
        *highs, *states, wide_misc, mom_in, mom_hid, mom_bias, mom_out,
    )


def solution(mesh):
    cells = mesh.shape["region"]
    inner = 8 if cells % 8 == 0 and cells > 8 else 2
    return jax.shard_map(
        functools.partial(body, inner),
        mesh=mesh,
        in_specs=(
            P("region", None, "batch"),
            P("region", "batch"),
            P("region", "batch"),
            P("batch", None),
            P(None, "batch"),
            P("region", "batch", None),
            P("region", None, "batch", None),
            P("region", None, "batch"),
            P("region", None, "batch"),
            P(None, "region", "batch", None),
            P(None, "region", None, "batch", None),
            P(None, "region", None, "batch"),
            P(None, "region", None, "batch"),
        ),
        out_specs=(
            P("region", None, None),
            P("region", None, None, None),
            P("region", None, None),
            P("region", None, None),
            P(None, "region", "batch", None),
            P(None, "region", None, "batch", None),
            P(None, "region", None, "batch"),
            P(None, "region", None, "batch"),
        ),
        check_vma=False,
    )
```

```python
import functools

import jax
import jax.numpy as jnp
from jax import lax
from jax.experimental import pallas as pl
from jax.experimental.pallas import tpu as pltpu
from jax.sharding import PartitionSpec as P

ENC = 63
HID = 256
S = 64
N_BATCH = 4
CHUNK = 4096
MIB = 1 << 20
LIMIT = 24

beta_first = 0.9
beta_second = 0.95
learn_rate = 0.01
norm_eps = 1e-06
adam_eps = 1e-08

f32 = jnp.float32
bf16 = jnp.bfloat16

ROWS_IN = HID // 16
ROWS_HID = HID // N_BATCH
MISC = ROWS_IN + 2 * ROWS_HID
BLOCK = MISC + 16


def dot(left, right):
    return lax.dot_general(left, right, (((1,), (0,)), ((), ())), preferred_element_type=f32)


def dot_last(left, right):
    return lax.dot_general(left, right, (((1,), (1,)), ((), ())), preferred_element_type=f32)


def at_own_lanes(rows, own):
    source = lax.broadcasted_iota(jnp.int32, (ROWS_HID, HID), 0)
    lane = lax.broadcasted_iota(jnp.int32, (ROWS_HID, HID), 1)
    place = jnp.where(lane == source + own * ROWS_HID, 1.0, 0.0).astype(bf16)
    return dot(rows, place).astype(bf16)


def pack_weights(w_in, w_hid, b_hid, w_out, out):
    out[0:ROWS_IN, :] = w_in[0].astype(bf16)
    for layer in range(2):
        at = ROWS_IN + layer * ROWS_HID
        out[at : at + ROWS_HID, :] = w_hid[0, layer].astype(bf16)
    bias = b_hid[0]
    top = bias.astype(bf16).astype(f32)
    middle = (bias - top).astype(bf16).astype(f32)
    rest = bias - top - middle
    rows = jnp.concatenate(
        [w_out[0], top, middle, rest, jnp.zeros((6, ROWS_HID), f32)], axis=0
    ).astype(bf16)
    out[MISC:BLOCK, :] = at_own_lanes(rows, lax.axis_index("batch"))


def by_lane(rows):
    ray = lax.broadcasted_iota(jnp.int32, (128, 128), 0)
    lane = lax.broadcasted_iota(jnp.int32, (128, 128), 1)
    place = jnp.where(ray == jnp.where(lane < S, 2 * lane, 2 * (lane - S) + 1), 1.0, 0.0)
    return dot(rows.astype(bf16), place.astype(bf16))


def prepare_kernel(
    w_in, w_hid, w_out, mom_in, mom_hid, mom_bias, mom_out, spacing, counts, ranks, target,
    out, gaps, live_counts, order, goal,
):
    own = lax.axis_index("batch")

    def low(value):
        return (value - value.astype(bf16).astype(f32)).astype(bf16)

    out[0:ROWS_IN, :] = low(w_in[0])
    for layer in range(2):
        at = ROWS_IN + layer * ROWS_HID
        out[at : at + ROWS_HID, :] = low(w_hid[0, layer])
    rest = w_out[0] - w_out[0].astype(bf16).astype(f32)
    rows = jnp.concatenate([rest, jnp.zeros((12, ROWS_HID), f32)], axis=0)
    out[MISC:BLOCK, :] = at_own_lanes(rows.astype(bf16), own)
    for moment in range(2):
        base = BLOCK * (moment + 1)
        out[base : base + ROWS_IN, :] = mom_in[moment, 0].astype(bf16)
        for layer in range(2):
            at = base + ROWS_IN + layer * ROWS_HID
            out[at : at + ROWS_HID, :] = mom_hid[moment, 0, layer].astype(bf16)
        rows = jnp.concatenate(
            [mom_out[moment, 0], mom_bias[moment, 0], jnp.zeros((10, ROWS_HID), f32)], axis=0
        )
        out[base + MISC : base + BLOCK, :] = at_own_lanes(rows.astype(bf16), own)

    gaps[...] = turn(spacing[...])
    order[...] = by_lane(ranks[...].astype(f32))
    top = target[...].astype(bf16).astype(f32)
    middle = (target[...] - top).astype(bf16).astype(f32)
    rest = target[...] - top - middle
    number = counts[...].astype(f32)
    moved = by_lane(jnp.concatenate([top, middle, rest, number, jnp.zeros((6, 128), f32)], axis=0))
    goal[...] = moved[0:3] + moved[3:6] + moved[6:9]
    live_counts[...] = moved[9:10]


def turn(rows):
    turned = jnp.concatenate([rows, rows], axis=0).T
    lane = lax.broadcasted_iota(jnp.int32, (S, 2 * S), 1)
    return jnp.where(lane < S, turned[:S], turned[S:])


def running_sum(values):
    row = lax.broadcasted_iota(jnp.int32, values.shape, 0)
    step = 1
    while step < S:
        values = values + jnp.where(row >= step, pltpu.roll(values, step, 0), 0.0)
        step *= 2
    return values


def one_minus_exp(depth):
    small = depth * (1.0 - depth * (0.5 - depth * (1.0 / 6.0 - depth * (1.0 / 24.0 - depth * (1.0 / 120.0)))))
    return jnp.where(depth < 0.1, small, 1.0 - jnp.exp(-depth))


def rectified(value):
    return jnp.maximum(value.astype(bf16), jnp.zeros((), bf16))


def sigmoid(value):
    return 1.0 / (1.0 + jnp.exp(-value))


def forward_kernel(
    own, from_one, from_two, from_three, feats, gaps, counts,
    act_one, act_two, act_three, wide_hid, wide_misc, shading, summary,
    wide_in, turned_in, turned_hid, bias_cols, out_rows, heads_rows,
):
    me = lax.axis_index("batch")
    misc = jnp.zeros((16, HID), f32)
    for back, block in enumerate((own, from_one, from_two, from_three)):
        owner = lax.rem(me + N_BATCH - back, N_BATCH)
        wide_in[pl.ds(pl.multiple_of(owner * ROWS_IN, 16), ROWS_IN), :] = block[0:ROWS_IN, :]
        for layer in range(2):
            at = ROWS_IN + layer * ROWS_HID
            wide_hid[layer, pl.ds(pl.multiple_of(owner * ROWS_HID, 16), ROWS_HID), :] = block[
                at : at + ROWS_HID, :
            ]
        misc = misc + block[MISC:BLOCK, :].astype(f32)
    wide_misc[...] = misc
    turned_in[...] = wide_in[...].astype(f32).T.astype(bf16)
    for layer in range(2):
        turned_hid[layer] = wide_hid[layer].astype(f32).T.astype(bf16)
    bias = misc[4:6] + misc[6:8] + misc[8:10]
    bias_cols[...] = jnp.concatenate([bias, jnp.zeros((6, HID), f32)], axis=0).T
    row = lax.broadcasted_iota(jnp.int32, (16, HID), 0)
    out_rows[...] = jnp.where(row < 4, misc, 0.0).astype(bf16)

    @pl.loop(0, feats.shape[1] // CHUNK)
    def _(step):
        columns = pl.ds(pl.multiple_of(step * CHUNK, CHUNK), CHUNK)
        one = rectified(dot(turned_in[...], feats[:, columns]))
        act_one[:, columns] = one
        two = rectified(dot(turned_hid[0], one) + bias_cols[:, 0:1])
        act_two[:, columns] = two
        three = rectified(dot(turned_hid[1], two) + bias_cols[:, 1:2])
        act_three[:, columns] = three
        heads = dot(out_rows[...], three)
        for tile in range(CHUNK // 128):
            at = pl.multiple_of((step * (CHUNK // 128) + tile) * 8, 8)
            heads_rows[pl.ds(at, 8), :] = heads[0:8, tile * 128 : (tile + 1) * 128]

    density = turn(heads_rows[pl.ds(0, S, stride=8), :])
    slot = lax.broadcasted_iota(jnp.int32, (S, 128), 0).astype(f32)
    live_gap = jnp.where(slot < counts[...], gaps[...], 0.0)
    soft = jnp.maximum(density, 0.0) + jnp.log1p(jnp.exp(-jnp.abs(density)))
    depth = soft * live_gap
    total = running_sum(depth)
    weight = jnp.exp(-(total - depth)) * one_minus_exp(depth)
    for channel in range(3):
        colour = sigmoid(turn(heads_rows[pl.ds(channel + 1, S, stride=8), :]))
        shading[channel] = colour
        summary[channel : channel + 1, :] = jnp.sum(weight * colour, axis=0, keepdims=True)
    summary[3:4, :] = -total[S - 1 : S]
    shading[3] = weight
    shading[4] = jnp.exp(-total)
    shading[5] = live_gap * sigmoid(density)


def composite(table, ranks, target, shading, reach_rows, grad_rows):
    cells = ranks.shape[0]
    order = ranks[...]
    own = lax.axis_index("region")
    prefix = jnp.zeros((cells, 128), f32)
    for cell in range(cells):
        prefix = prefix + jnp.where(
            ranks[cell : cell + 1, :] < order, table[4 * cell + 3 : 4 * cell + 4, :], 0.0
        )
    reach = jnp.exp(prefix)
    reach_rows[...] = reach
    own_reach = reach_rows[pl.ds(own, 1), :]
    later = order > ranks[pl.ds(own, 1), :]
    grad_seg = []
    grad_log = jnp.zeros((1, 128), f32)
    for channel in range(3):
        lit = reach * table[pl.ds(channel, cells, stride=4), :]
        grad_colour = 2.0 * (jnp.sum(lit, axis=0, keepdims=True) - target[channel : channel + 1, :])
        behind = jnp.sum(jnp.where(later, lit, 0.0), axis=0, keepdims=True)
        grad_log = grad_log + grad_colour * behind
        grad_seg.append(own_reach * grad_colour)
    weight = shading[3]
    emit = grad_seg[0] * shading[0] + grad_seg[1] * shading[1] + grad_seg[2] * shading[2]
    carried = emit * weight
    running = running_sum(carried)
    after = running[S - 1 : S] - running
    grad_depth = emit * shading[4] - after - grad_log
    grad_rows[...] = jnp.zeros(grad_rows.shape, f32)
    grad_rows[pl.ds(0, S, stride=16), :] = turn(grad_depth * shading[5])
    for channel in range(3):
        colour = shading[channel]
        shade = grad_seg[channel] * weight * colour * (1.0 - colour)
        grad_rows[pl.ds(channel + 1, S, stride=16), :] = turn(shade)


def masked(act, back):
    return jnp.where(act > 0, back.astype(bf16), jnp.zeros((), bf16))


def backward_kernel(
    table, ranks, target, shading, wide_hid, wide_misc, feats, act_one, act_two, act_three,
    even, odd,
    reach_rows, grad_rows, out_cols, sum_third, sum_second, sum_first, sum_out,
):
    composite(table, ranks, target, shading, reach_rows, grad_rows)
    row = lax.broadcasted_iota(jnp.int32, (16, HID), 0)
    out_cols[...] = jnp.where(row < 4, wide_misc[...], 0.0).T.astype(bf16)
    for total in (sum_third, sum_second, sum_first, sum_out):
        total[...] = jnp.zeros(total.shape, f32)

    @pl.loop(0, feats.shape[1] // CHUNK)
    def _(step):
        columns = pl.ds(pl.multiple_of(step * CHUNK, CHUNK), CHUNK)
        tiles = CHUNK // 128
        heads = jnp.concatenate(
            [
                grad_rows[pl.ds(pl.multiple_of((step * tiles + tile) * 16, 16), 16), :]
                for tile in range(tiles)
            ],
            axis=1,
        ).astype(bf16)
        ones = jnp.ones((16, CHUNK), bf16)
        one, two, three = act_one[:, columns], act_two[:, columns], act_three[:, columns]
        back_three = masked(three, dot(out_cols[...], heads))
        sum_out[...] += dot_last(heads, three)
        back_two = masked(two, dot(wide_hid[1], back_three))
        sum_third[...] += dot_last(jnp.concatenate([two, ones], axis=0), back_three)
        back_one = masked(one, dot(wide_hid[0], back_two))
        sum_second[...] += dot_last(jnp.concatenate([one, ones], axis=0), back_two)
        sum_first[...] += dot_last(feats[:, columns], back_one)

    misc = jnp.where(row < 4, sum_out[...], 0.0)
    misc = misc + jnp.where(row == 4, sum_second[HID : HID + 16, :], 0.0)
    misc = misc + jnp.where(row == 5, sum_third[HID : HID + 16, :], 0.0)
    even[0:HID, :] = sum_third[0:HID, :].astype(bf16)
    even[HID : HID + 32, :] = sum_first[0:32, :].astype(bf16)
    even[HID + 32 : HID + 48, :] = misc.astype(bf16)
    odd[0:HID, :] = sum_second[0:HID, :].astype(bf16)
    odd[HID : HID + 32, :] = sum_first[32:64, :].astype(bf16)


def pair_kernel(even, even_other, odd, odd_other, even_sum, odd_sum):
    even_sum[...] = (even[...].astype(f32) + even_other[...].astype(f32)).astype(bf16)
    odd_sum[...] = (odd[...].astype(f32) + odd_other[...].astype(f32)).astype(bf16)


def adam(grad, first, second, scale):
    scaled = grad * scale
    first = beta_first * first + (1.0 - beta_first) * scaled
    second = beta_second * second + (1.0 - beta_second) * scaled * scaled
    return first, second, learn_rate * first / (jnp.sqrt(second) + adam_eps)


def update_kernel(
    even, even_other, odd, odd_other,
    high_0, high_1, high_2, high_3,
    state_0, state_1, state_2, state_3,
    wide_misc, mom_in, mom_hid, mom_bias, mom_out,
    new_in, new_hid, new_bias, new_out,
    out_in, out_hid, out_bias, out_out,
    upper, lower, first_rows,
):
    me = lax.axis_index("batch")
    param_count = (ENC + 1) * HID + 2 * HID * HID + 6 * HID
    upper[...] = even[...].astype(f32) + even_other[...].astype(f32)
    lower[...] = odd[...].astype(f32) + odd_other[...].astype(f32)
    first_rows[0:32, :] = upper[HID : HID + 32, :]
    first_rows[32:64, :] = lower[HID : HID + 32, :]
    grad_misc = upper[HID + 32 : HID + 48, :]
    squares = jnp.sum(upper[...] * upper[...], axis=0, keepdims=True) + jnp.sum(
        lower[...] * lower[...], axis=0, keepdims=True
    )
    total = jnp.sum(squares, axis=1, keepdims=True)
    scale = lax.rsqrt(total / param_count + norm_eps)

    def fresh(grad, high, state, at, rows):
        _, _, change = adam(
            grad,
            state[BLOCK + at : BLOCK + at + rows, :].astype(f32),
            state[2 * BLOCK + at : 2 * BLOCK + at + rows, :].astype(f32),
            scale,
        )
        value = high[at : at + rows, :].astype(f32) + state[at : at + rows, :].astype(f32)
        return value - change

    highs = (high_0, high_1, high_2, high_3)
    states = (state_0, state_1, state_2, state_3)
    low_misc = jnp.zeros((16, HID), f32)
    first_misc = jnp.zeros((16, HID), f32)
    second_misc = jnp.zeros((16, HID), f32)
    for back in range(N_BATCH):
        owner = lax.rem(me + N_BATCH - back, N_BATCH)
        high, state = highs[back], states[back]
        hid = pl.ds(pl.multiple_of(owner * ROWS_HID, 16), ROWS_HID)
        new_hid[0, 0, hid, :] = fresh(lower[hid, :], high, state, ROWS_IN, ROWS_HID)
        new_hid[0, 1, hid, :] = fresh(upper[hid, :], high, state, ROWS_IN + ROWS_HID, ROWS_HID)
        first = pl.ds(pl.multiple_of(owner * ROWS_IN, 16), ROWS_IN)
        grad = first_rows[first, :]
        new_in[0, first, :] = fresh(grad, high, state, 0, ROWS_IN)
        low_misc = low_misc + state[MISC:BLOCK, :].astype(f32)
        first_misc = first_misc + state[BLOCK + MISC : 2 * BLOCK, :].astype(f32)
        second_misc = second_misc + state[2 * BLOCK + MISC : 3 * BLOCK, :].astype(f32)

    _, _, change = adam(grad_misc, first_misc, second_misc, scale)
    weights = wide_misc[...]
    new_out[0] = weights[0:4] + low_misc[0:4] - change[0:4]
    new_bias[0] = weights[4:6] + weights[6:8] + weights[8:10] - change[4:6]

    own = pl.ds(pl.multiple_of(me * ROWS_HID, 16), ROWS_HID)
    for layer, grads in ((0, lower), (1, upper)):
        moments = adam(grads[own, :], mom_hid[0, 0, layer], mom_hid[1, 0, layer], scale)
        out_hid[0, 0, layer] = moments[0]
        out_hid[1, 0, layer] = moments[1]
    grad = first_rows[pl.ds(pl.multiple_of(me * ROWS_IN, 16), ROWS_IN), :]
    moments = adam(grad, mom_in[0, 0], mom_in[1, 0], scale)
    out_in[0, 0] = moments[0]
    out_in[1, 0] = moments[1]
    own_misc = jnp.zeros((16, ROWS_HID), f32)
    for owner in range(N_BATCH):
        part = grad_misc[:, owner * ROWS_HID : (owner + 1) * ROWS_HID]
        own_misc = own_misc + jnp.where(me == owner, part, 0.0)
    moments = adam(own_misc[0:4], mom_out[0, 0], mom_out[1, 0], scale)
    out_out[0, 0] = moments[0]
    out_out[1, 0] = moments[1]
    moments = adam(own_misc[4:6], mom_bias[0, 0], mom_bias[1, 0], scale)
    out_bias[0, 0] = moments[0]
    out_bias[1, 0] = moments[1]


def fetched(kernel, fetch, outs):
    def run(*refs):
        sources, rest = refs[:fetch], refs[fetch : fetch + outs]
        copies, sem = refs[fetch + outs : -1], refs[-1]
        moves = [pltpu.make_async_copy(a, b, sem.at[i]) for i, (a, b) in enumerate(zip(sources, copies))]
        for move in moves:
            move.start()
        for move in moves:
            move.wait()
        kernel(*copies, *rest)

    return run


def call_on_hbm(kernel, outs, name, *arrays):
    outs = outs if isinstance(outs, tuple) else (outs,)
    return pl.pallas_call(
        fetched(kernel, len(arrays), len(outs)),
        out_shape=outs,
        in_specs=[pl.BlockSpec(memory_space=pltpu.HBM)] * len(arrays),
        scratch_shapes=[pltpu.VMEM(a.shape, a.dtype) for a in arrays]
        + [pltpu.SemaphoreType.DMA((len(arrays),))],
        compiler_params=pltpu.CompilerParams(vmem_limit_bytes=60 * MIB),
        name=name,
    )(*arrays)


def call(kernel, outs, scratch=(), name=None):
    return pl.pallas_call(
        kernel,
        out_shape=outs,
        scratch_shapes=[pltpu.VMEM(*s) for s in scratch],
        compiler_params=pltpu.CompilerParams(vmem_limit_bytes=LIMIT * MIB),
        name=name,
    )


def from_others(block):
    return [
        lax.ppermute(block, "batch", [(i, (i + hop) % N_BATCH) for i in range(N_BATCH)])
        for hop in (1, 2, 3)
    ]


def swapped(block, first):
    pairs = [(0, 1), (2, 3)] if first else [(1, 2), (3, 0)]
    return lax.ppermute(block, "batch", pairs + [(j, i) for i, j in pairs])


def held(dims, dtype=f32):
    return pltpu.VMEM(dims, dtype)


def shape(dims, dtype=f32):
    return jax.ShapeDtypeStruct(dims, dtype)


def body(
    inner,
    features, spacing, counts, depth_rank, target,
    w_in, w_hid, b_hid, w_out,
    mom_in, mom_hid, mom_bias, mom_out,
):
    samples = features.shape[2]
    rays = samples // S
    cells = depth_rank.shape[1]
    outer = cells // inner

    (block,) = call_on_hbm(
        pack_weights, held((BLOCK, HID), bf16), "pack_weights", w_in, w_hid, b_hid, w_out
    )
    block, spacing = lax.optimization_barrier((block, spacing))
    highs = [block] + from_others(block)
    state, gaps, live_counts, ranks, goal = call_on_hbm(
        prepare_kernel,
        (
            held((3 * BLOCK, HID), bf16), held((S, rays)), held((1, rays)), held((cells, rays)),
            held((3, rays)),
        ),
        "prepare",
        w_in, w_hid, w_out, mom_in, mom_hid, mom_bias, mom_out,
        spacing.reshape(rays // 2, 2 * S), counts, depth_rank.T, target,
    )
    feats = jnp.concatenate([features[0], jnp.ones((1, samples), bf16)], axis=0)
    state, feats, *highs[1:] = lax.optimization_barrier((state, feats, *highs[1:]))
    states = [state] + from_others(state)

    act = held((HID, samples), bf16)
    act_one, act_two, act_three, wide_hid, wide_misc, shading, summary = call(
        forward_kernel,
        (
            act, act, act, held((2, HID, HID), bf16),
            held((16, HID)), held((6, S, 128)), held((4, rays)),
        ),
        scratch=[
            ((ENC + 1, HID), bf16), ((HID, ENC + 1), bf16), ((2, HID, HID), bf16), ((HID, 8), f32),
            ((16, HID), bf16), ((samples // 16, 128), f32),
        ],
        name="forward",
    )(*highs, feats, gaps, live_counts)

    near = [[z * inner + i for i in range(inner)] for z in range(outer)]
    far = [[z * inner + i for z in range(outer)] for i in range(inner)]
    some = lax.all_to_all(
        jnp.broadcast_to(summary[None], (inner, 4, rays)), "region", 0, 0,
        axis_index_groups=near, tiled=True,
    )
    some, *states = lax.optimization_barrier((some, *states))
    table = lax.all_to_all(
        jnp.broadcast_to(some[None], (outer, inner, 4, rays)), "region", 0, 0,
        axis_index_groups=far, tiled=True,
    ).reshape(cells * 4, rays)

    even, odd = call(
        backward_kernel,
        (held((HID + 48, HID), bf16), held((HID + 32, HID), bf16)),
        scratch=[
            ((cells, 128), f32), ((samples // 8, 128), f32), ((HID, 16), bf16), ((HID + 16, HID), f32),
            ((HID + 16, HID), f32), ((64, HID), f32), ((16, HID), f32),
        ],
        name="backward",
    )(table, ranks, goal, shading, wide_hid, wide_misc, feats, act_one, act_two, act_three)
    even, odd = call(
        pair_kernel, (held(even.shape, bf16), held(odd.shape, bf16)), name="pair"
    )(even, swapped(even, True), odd, swapped(odd, False))

    return call(
        update_kernel,
        (
            shape((1, ENC + 1, HID)), shape((1, 2, HID, HID)), shape((1, 2, HID)), shape((1, 4, HID)),
            shape(mom_in.shape), shape(mom_hid.shape), shape(mom_bias.shape), shape(mom_out.shape),
        ),
        scratch=[((HID + 48, HID), f32), ((HID + 32, HID), f32), ((64, HID), f32)],
        name="update",
    )(
        even, swapped(even, False), odd, swapped(odd, True),
        *highs, *states, wide_misc, mom_in, mom_hid, mom_bias, mom_out,
    )


def solution(mesh):
    cells = mesh.shape["region"]
    inner = 8 if cells % 8 == 0 and cells > 8 else 2
    return jax.shard_map(
        functools.partial(body, inner),
        mesh=mesh,
        in_specs=(
            P("region", None, "batch"),
            P("region", "batch"),
            P("region", "batch"),
            P("batch", None),
            P(None, "batch"),
            P("region", "batch", None),
            P("region", None, "batch", None),
            P("region", None, "batch"),
            P("region", None, "batch"),
            P(None, "region", "batch", None),
            P(None, "region", None, "batch", None),
            P(None, "region", None, "batch"),
            P(None, "region", None, "batch"),
        ),
        out_specs=(
            P("region", None, None),
            P("region", None, None, None),
            P("region", None, None),
            P("region", None, None),
            P(None, "region", "batch", None),
            P(None, "region", None, "batch", None),
            P(None, "region", None, "batch"),
            P(None, "region", None, "batch"),
        ),
        check_vma=False,
    )
```

```python
import jax
import jax.numpy as jnp
from jax import lax
from jax.experimental import pallas as pl
from jax.experimental.pallas import tpu as pltpu
from jax.sharding import PartitionSpec as P

ENC = 63
HID = 256
S = 64
N_BATCH = 4
CHUNK = 8192
MIB = 1 << 20
LIMIT = 24

beta_first = 0.9
beta_second = 0.95
learn_rate = 0.01
norm_eps = 1e-06
adam_eps = 1e-08

f32 = jnp.float32
bf16 = jnp.bfloat16

ROWS_IN = HID // 16
ROWS_HID = HID // N_BATCH
MISC = ROWS_IN + 2 * ROWS_HID
BLOCK = MISC + 16


def dot(left, right):
    return lax.dot_general(left, right, (((1,), (0,)), ((), ())), preferred_element_type=f32)


def dot_last(left, right):
    return lax.dot_general(left, right, (((1,), (1,)), ((), ())), preferred_element_type=f32)


def at_own_lanes(rows, own):
    source = lax.broadcasted_iota(jnp.int32, (ROWS_HID, HID), 0)
    lane = lax.broadcasted_iota(jnp.int32, (ROWS_HID, HID), 1)
    place = jnp.where(lane == source + own * ROWS_HID, 1.0, 0.0).astype(bf16)
    return dot(rows, place).astype(bf16)


def pack_weights(w_in, w_hid, b_hid, w_out, out):
    out[0:ROWS_IN, :] = w_in[0].astype(bf16)
    for layer in range(2):
        at = ROWS_IN + layer * ROWS_HID
        out[at : at + ROWS_HID, :] = w_hid[0, layer].astype(bf16)
    bias = b_hid[0]
    top = bias.astype(bf16).astype(f32)
    middle = (bias - top).astype(bf16).astype(f32)
    rest = bias - top - middle
    rows = jnp.concatenate(
        [w_out[0], top, middle, rest, jnp.zeros((6, ROWS_HID), f32)], axis=0
    ).astype(bf16)
    out[MISC:BLOCK, :] = at_own_lanes(rows, lax.axis_index("batch"))


def by_lane(rows):
    ray = lax.broadcasted_iota(jnp.int32, (128, 128), 0)
    lane = lax.broadcasted_iota(jnp.int32, (128, 128), 1)
    place = jnp.where(ray == jnp.where(lane < S, 2 * lane, 2 * (lane - S) + 1), 1.0, 0.0)
    return dot(rows.astype(bf16), place.astype(bf16))


def prepare_kernel(
    w_in, w_hid, w_out, mom_in, mom_hid, mom_bias, mom_out, spacing, counts, ranks, target,
    out, gaps, live_counts, order, goal,
):
    own = lax.axis_index("batch")

    def low(value):
        return (value - value.astype(bf16).astype(f32)).astype(bf16)

    out[0:ROWS_IN, :] = low(w_in[0])
    for layer in range(2):
        at = ROWS_IN + layer * ROWS_HID
        out[at : at + ROWS_HID, :] = low(w_hid[0, layer])
    rest = w_out[0] - w_out[0].astype(bf16).astype(f32)
    rows = jnp.concatenate([rest, jnp.zeros((12, ROWS_HID), f32)], axis=0)
    out[MISC:BLOCK, :] = at_own_lanes(rows.astype(bf16), own)
    for moment in range(2):
        base = BLOCK * (moment + 1)
        out[base : base + ROWS_IN, :] = mom_in[moment, 0].astype(bf16)
        for layer in range(2):
            at = base + ROWS_IN + layer * ROWS_HID
            out[at : at + ROWS_HID, :] = mom_hid[moment, 0, layer].astype(bf16)
        rows = jnp.concatenate(
            [mom_out[moment, 0], mom_bias[moment, 0], jnp.zeros((10, ROWS_HID), f32)], axis=0
        )
        out[base + MISC : base + BLOCK, :] = at_own_lanes(rows.astype(bf16), own)

    gaps[...] = turn(spacing[...])
    order[...] = by_lane(ranks[...].astype(f32))
    top = target[...].astype(bf16).astype(f32)
    middle = (target[...] - top).astype(bf16).astype(f32)
    rest = target[...] - top - middle
    number = counts[...].astype(f32)
    moved = by_lane(jnp.concatenate([top, middle, rest, number, jnp.zeros((6, 128), f32)], axis=0))
    goal[...] = moved[0:3] + moved[3:6] + moved[6:9]
    live_counts[...] = moved[9:10]


def turn(rows):
    turned = jnp.concatenate([rows, rows], axis=0).T
    lane = lax.broadcasted_iota(jnp.int32, (S, 2 * S), 1)
    return jnp.where(lane < S, turned[:S], turned[S:])


def running_sum(values):
    row = lax.broadcasted_iota(jnp.int32, values.shape, 0)
    step = 1
    while step < S:
        values = values + jnp.where(row >= step, pltpu.roll(values, step, 0), 0.0)
        step *= 2
    return values


def one_minus_exp(depth):
    small = depth * (1.0 - depth * (0.5 - depth * (1.0 / 6.0 - depth * (1.0 / 24.0 - depth * (1.0 / 120.0)))))
    return jnp.where(depth < 0.1, small, 1.0 - jnp.exp(-depth))


def rectified(value):
    return jnp.maximum(value.astype(bf16), jnp.zeros((), bf16))


def sigmoid(value):
    return 1.0 / (1.0 + jnp.exp(-value))


def forward_kernel(
    own, from_one, from_two, from_three, feats, gaps, counts,
    act_one, act_two, act_three, wide_hid, wide_misc, shading, summary,
    wide_in, turned_in, turned_hid, bias_cols, out_rows, heads_rows,
):
    me = lax.axis_index("batch")
    misc = jnp.zeros((16, HID), f32)
    for back, block in enumerate((own, from_one, from_two, from_three)):
        owner = lax.rem(me + N_BATCH - back, N_BATCH)
        wide_in[pl.ds(pl.multiple_of(owner * ROWS_IN, 16), ROWS_IN), :] = block[0:ROWS_IN, :]
        for layer in range(2):
            at = ROWS_IN + layer * ROWS_HID
            wide_hid[layer, pl.ds(pl.multiple_of(owner * ROWS_HID, 16), ROWS_HID), :] = block[
                at : at + ROWS_HID, :
            ]
        misc = misc + block[MISC:BLOCK, :].astype(f32)
    wide_misc[...] = misc
    turned_in[...] = wide_in[...].astype(f32).T.astype(bf16)
    for layer in range(2):
        turned_hid[layer] = wide_hid[layer].astype(f32).T.astype(bf16)
    bias = misc[4:6] + misc[6:8] + misc[8:10]
    bias_cols[...] = jnp.concatenate([bias, jnp.zeros((6, HID), f32)], axis=0).T
    row = lax.broadcasted_iota(jnp.int32, (16, HID), 0)
    out_rows[...] = jnp.where(row < 4, misc, 0.0).astype(bf16)

    @pl.loop(0, feats.shape[1] // CHUNK)
    def _(step):
        columns = pl.ds(pl.multiple_of(step * CHUNK, CHUNK), CHUNK)
        one = rectified(dot(turned_in[...], feats[:, columns]))
        act_one[:, columns] = one
        two = rectified(dot(turned_hid[0], one) + bias_cols[:, 0:1])
        act_two[:, columns] = two
        three = rectified(dot(turned_hid[1], two) + bias_cols[:, 1:2])
        act_three[:, columns] = three
        heads = dot(out_rows[...], three)
        for tile in range(CHUNK // 128):
            at = pl.multiple_of((step * (CHUNK // 128) + tile) * 8, 8)
            heads_rows[pl.ds(at, 8), :] = heads[0:8, tile * 128 : (tile + 1) * 128]

    density = turn(heads_rows[pl.ds(0, S, stride=8), :])
    slot = lax.broadcasted_iota(jnp.int32, (S, 128), 0).astype(f32)
    live_gap = jnp.where(slot < counts[...], gaps[...], 0.0)
    soft = jnp.maximum(density, 0.0) + jnp.log1p(jnp.exp(-jnp.abs(density)))
    depth = soft * live_gap
    total = running_sum(depth)
    weight = jnp.exp(-(total - depth)) * one_minus_exp(depth)
    for channel in range(3):
        colour = sigmoid(turn(heads_rows[pl.ds(channel + 1, S, stride=8), :]))
        shading[channel] = colour
        summary[channel : channel + 1, :] = jnp.sum(weight * colour, axis=0, keepdims=True)
    summary[3:4, :] = -total[S - 1 : S]
    shading[3] = weight
    shading[4] = jnp.exp(-total)
    shading[5] = live_gap * sigmoid(density)


def composite(table, ranks, target, shading, reach_rows, grad_rows):
    cells = ranks.shape[0]
    order = ranks[...]
    own = lax.axis_index("region")
    prefix = jnp.zeros((cells, 128), f32)
    for cell in range(cells):
        prefix = prefix + jnp.where(
            ranks[cell : cell + 1, :] < order, table[4 * cell + 3 : 4 * cell + 4, :], 0.0
        )
    reach = jnp.exp(prefix)
    reach_rows[...] = reach
    own_reach = reach_rows[pl.ds(own, 1), :]
    later = order > ranks[pl.ds(own, 1), :]
    grad_seg = []
    grad_log = jnp.zeros((1, 128), f32)
    for channel in range(3):
        lit = reach * table[pl.ds(channel, cells, stride=4), :]
        grad_colour = 2.0 * (jnp.sum(lit, axis=0, keepdims=True) - target[channel : channel + 1, :])
        behind = jnp.sum(jnp.where(later, lit, 0.0), axis=0, keepdims=True)
        grad_log = grad_log + grad_colour * behind
        grad_seg.append(own_reach * grad_colour)
    weight = shading[3]
    emit = grad_seg[0] * shading[0] + grad_seg[1] * shading[1] + grad_seg[2] * shading[2]
    carried = emit * weight
    running = running_sum(carried)
    after = running[S - 1 : S] - running
    grad_depth = emit * shading[4] - after - grad_log
    grad_rows[...] = jnp.zeros(grad_rows.shape, f32)
    grad_rows[pl.ds(0, S, stride=16), :] = turn(grad_depth * shading[5])
    for channel in range(3):
        colour = shading[channel]
        shade = grad_seg[channel] * weight * colour * (1.0 - colour)
        grad_rows[pl.ds(channel + 1, S, stride=16), :] = turn(shade)


def masked(act, back):
    return jnp.where(act > 0, back.astype(bf16), jnp.zeros((), bf16))


def backward_kernel(
    table, ranks, target, shading, wide_hid, wide_misc, feats, act_one, act_two, act_three,
    even, odd,
    reach_rows, grad_rows, out_cols, sum_third, sum_second, sum_first, sum_out,
):
    composite(table, ranks, target, shading, reach_rows, grad_rows)
    row = lax.broadcasted_iota(jnp.int32, (16, HID), 0)
    out_cols[...] = jnp.where(row < 4, wide_misc[...], 0.0).T.astype(bf16)
    for total in (sum_third, sum_second, sum_first, sum_out):
        total[...] = jnp.zeros(total.shape, f32)

    @pl.loop(0, feats.shape[1] // CHUNK)
    def _(step):
        columns = pl.ds(pl.multiple_of(step * CHUNK, CHUNK), CHUNK)
        tiles = CHUNK // 128
        heads = jnp.concatenate(
            [
                grad_rows[pl.ds(pl.multiple_of((step * tiles + tile) * 16, 16), 16), :]
                for tile in range(tiles)
            ],
            axis=1,
        ).astype(bf16)
        ones = jnp.ones((16, CHUNK), bf16)
        one, two, three = act_one[:, columns], act_two[:, columns], act_three[:, columns]
        back_three = masked(three, dot(out_cols[...], heads))
        sum_out[...] += dot_last(heads, three)
        back_two = masked(two, dot(wide_hid[1], back_three))
        sum_third[...] += dot_last(jnp.concatenate([two, ones], axis=0), back_three)
        back_one = masked(one, dot(wide_hid[0], back_two))
        sum_second[...] += dot_last(jnp.concatenate([one, ones], axis=0), back_two)
        sum_first[...] += dot_last(feats[:, columns], back_one)

    misc = jnp.where(row < 4, sum_out[...], 0.0)
    misc = misc + jnp.where(row == 4, sum_second[HID : HID + 16, :], 0.0)
    misc = misc + jnp.where(row == 5, sum_third[HID : HID + 16, :], 0.0)
    even[0:HID, :] = sum_third[0:HID, :].astype(bf16)
    even[HID : HID + 32, :] = sum_first[0:32, :].astype(bf16)
    even[HID + 32 : HID + 48, :] = misc.astype(bf16)
    odd[0:HID, :] = sum_second[0:HID, :].astype(bf16)
    odd[HID : HID + 32, :] = sum_first[32:64, :].astype(bf16)


def pair_kernel(own, other, total):
    total[...] = (own[...].astype(f32) + other[...].astype(f32)).astype(bf16)


def adam(grad, first, second, scale):
    scaled = grad * scale
    first = beta_first * first + (1.0 - beta_first) * scaled
    second = beta_second * second + (1.0 - beta_second) * scaled * scaled
    return first, second, learn_rate * first / (jnp.sqrt(second) + adam_eps)


def update_kernel(
    even, even_other, odd, odd_other,
    high_0, high_1, high_2, high_3,
    state_0, state_1, state_2, state_3,
    wide_misc, mom_in, mom_hid, mom_bias, mom_out,
    new_in, new_hid, new_bias, new_out,
    out_in, out_hid, out_bias, out_out,
    upper, lower, first_rows,
):
    me = lax.axis_index("batch")
    param_count = (ENC + 1) * HID + 2 * HID * HID + 6 * HID
    upper[...] = even[...].astype(f32) + even_other[...].astype(f32)
    lower[...] = odd[...].astype(f32) + odd_other[...].astype(f32)
    first_rows[0:32, :] = upper[HID : HID + 32, :]
    first_rows[32:64, :] = lower[HID : HID + 32, :]
    grad_misc = upper[HID + 32 : HID + 48, :]
    squares = jnp.sum(upper[...] * upper[...], axis=0, keepdims=True) + jnp.sum(
        lower[...] * lower[...], axis=0, keepdims=True
    )
    total = jnp.sum(squares, axis=1, keepdims=True)
    scale = lax.rsqrt(total / param_count + norm_eps)

    def fresh(grad, high, state, at, rows):
        _, _, change = adam(
            grad,
            state[BLOCK + at : BLOCK + at + rows, :].astype(f32),
            state[2 * BLOCK + at : 2 * BLOCK + at + rows, :].astype(f32),
            scale,
        )
        value = high[at : at + rows, :].astype(f32) + state[at : at + rows, :].astype(f32)
        return value - change

    highs = (high_0, high_1, high_2, high_3)
    states = (state_0, state_1, state_2, state_3)
    low_misc = jnp.zeros((16, HID), f32)
    first_misc = jnp.zeros((16, HID), f32)
    second_misc = jnp.zeros((16, HID), f32)
    for back in range(N_BATCH):
        owner = lax.rem(me + N_BATCH - back, N_BATCH)
        high, state = highs[back], states[back]
        hid = pl.ds(pl.multiple_of(owner * ROWS_HID, 16), ROWS_HID)
        new_hid[0, 0, hid, :] = fresh(lower[hid, :], high, state, ROWS_IN, ROWS_HID)
        new_hid[0, 1, hid, :] = fresh(upper[hid, :], high, state, ROWS_IN + ROWS_HID, ROWS_HID)
        first = pl.ds(pl.multiple_of(owner * ROWS_IN, 16), ROWS_IN)
        grad = first_rows[first, :]
        new_in[0, first, :] = fresh(grad, high, state, 0, ROWS_IN)
        low_misc = low_misc + state[MISC:BLOCK, :].astype(f32)
        first_misc = first_misc + state[BLOCK + MISC : 2 * BLOCK, :].astype(f32)
        second_misc = second_misc + state[2 * BLOCK + MISC : 3 * BLOCK, :].astype(f32)

    _, _, change = adam(grad_misc, first_misc, second_misc, scale)
    weights = wide_misc[...]
    new_out[0] = weights[0:4] + low_misc[0:4] - change[0:4]
    new_bias[0] = weights[4:6] + weights[6:8] + weights[8:10] - change[4:6]

    own = pl.ds(pl.multiple_of(me * ROWS_HID, 16), ROWS_HID)
    for layer, grads in ((0, lower), (1, upper)):
        moments = adam(grads[own, :], mom_hid[0, 0, layer], mom_hid[1, 0, layer], scale)
        out_hid[0, 0, layer] = moments[0]
        out_hid[1, 0, layer] = moments[1]
    grad = first_rows[pl.ds(pl.multiple_of(me * ROWS_IN, 16), ROWS_IN), :]
    moments = adam(grad, mom_in[0, 0], mom_in[1, 0], scale)
    out_in[0, 0] = moments[0]
    out_in[1, 0] = moments[1]
    own_misc = jnp.zeros((16, ROWS_HID), f32)
    for owner in range(N_BATCH):
        part = grad_misc[:, owner * ROWS_HID : (owner + 1) * ROWS_HID]
        own_misc = own_misc + jnp.where(me == owner, part, 0.0)
    moments = adam(own_misc[0:4], mom_out[0, 0], mom_out[1, 0], scale)
    out_out[0, 0] = moments[0]
    out_out[1, 0] = moments[1]
    moments = adam(own_misc[4:6], mom_bias[0, 0], mom_bias[1, 0], scale)
    out_bias[0, 0] = moments[0]
    out_bias[1, 0] = moments[1]


def fetched(kernel, fetch, outs):
    def run(*refs):
        sources, rest = refs[:fetch], refs[fetch : fetch + outs]
        copies, sem = refs[fetch + outs : -1], refs[-1]
        moves = [pltpu.make_async_copy(a, b, sem.at[i]) for i, (a, b) in enumerate(zip(sources, copies))]
        for move in moves:
            move.start()
        for move in moves:
            move.wait()
        kernel(*copies, *rest)

    return run


def call_on_hbm(kernel, outs, name, *arrays):
    outs = outs if isinstance(outs, tuple) else (outs,)
    return pl.pallas_call(
        fetched(kernel, len(arrays), len(outs)),
        out_shape=outs,
        in_specs=[pl.BlockSpec(memory_space=pltpu.HBM)] * len(arrays),
        scratch_shapes=[pltpu.VMEM(a.shape, a.dtype) for a in arrays]
        + [pltpu.SemaphoreType.DMA((len(arrays),))],
        compiler_params=pltpu.CompilerParams(vmem_limit_bytes=60 * MIB),
        name=name,
    )(*arrays)


def call(kernel, outs, scratch=(), name=None):
    return pl.pallas_call(
        kernel,
        out_shape=outs,
        scratch_shapes=[pltpu.VMEM(*s) for s in scratch],
        compiler_params=pltpu.CompilerParams(vmem_limit_bytes=LIMIT * MIB),
        name=name,
    )


def from_others(block):
    return [
        lax.ppermute(block, "batch", [(i, (i + hop) % N_BATCH) for i in range(N_BATCH)])
        for hop in (1, 2, 3)
    ]


def swapped(block, first):
    pairs = [(0, 1), (2, 3)] if first else [(1, 2), (3, 0)]
    return lax.ppermute(block, "batch", pairs + [(j, i) for i, j in pairs])


def held(dims, dtype=f32):
    return pltpu.VMEM(dims, dtype)


def shape(dims, dtype=f32):
    return jax.ShapeDtypeStruct(dims, dtype)


def body(
    features, spacing, counts, depth_rank, target,
    w_in, w_hid, b_hid, w_out,
    mom_in, mom_hid, mom_bias, mom_out,
):
    samples = features.shape[2]
    rays = samples // S
    cells = depth_rank.shape[1]

    (block,) = call_on_hbm(
        pack_weights, held((BLOCK, HID), bf16), "pack_weights", w_in, w_hid, b_hid, w_out
    )
    block, spacing = lax.optimization_barrier((block, spacing))
    highs = [block] + from_others(block)
    state, gaps, live_counts, ranks, goal = call_on_hbm(
        prepare_kernel,
        (
            held((3 * BLOCK, HID), bf16), held((S, rays)), held((1, rays)), held((cells, rays)),
            held((3, rays)),
        ),
        "prepare",
        w_in, w_hid, w_out, mom_in, mom_hid, mom_bias, mom_out,
        spacing.reshape(rays // 2, 2 * S), counts, depth_rank.T, target,
    )
    feats = jnp.concatenate([features[0], jnp.ones((1, samples), bf16)], axis=0)
    state, feats, *highs[1:] = lax.optimization_barrier((state, feats, *highs[1:]))
    sides = [
        lax.ppermute(state, "batch", [(i, (i + hop) % N_BATCH) for i in range(N_BATCH)])
        for hop in (1, 3)
    ]

    act = held((HID, samples), bf16)
    act_one, act_two, act_three, wide_hid, wide_misc, shading, summary = call(
        forward_kernel,
        (
            act, act, act, held((2, HID, HID), bf16),
            held((16, HID)), held((6, S, 128)), held((4, rays)),
        ),
        scratch=[
            ((ENC + 1, HID), bf16), ((HID, ENC + 1), bf16), ((2, HID, HID), bf16), ((HID, 8), f32),
            ((16, HID), bf16), ((samples // 16, 128), f32),
        ],
        name="forward",
    )(*highs, feats, gaps, live_counts)

    summary, *sides = lax.optimization_barrier((summary, *sides))
    table = lax.all_to_all(
        jnp.broadcast_to(summary[None], (cells, 4, rays)), "region", 0, 0, tiled=True
    ).reshape(cells * 4, rays)
    table, state = lax.optimization_barrier((table, state))
    opposite = lax.ppermute(state, "batch", [(i, (i + 2) % N_BATCH) for i in range(N_BATCH)])

    even, odd = call(
        backward_kernel,
        (held((HID + 48, HID), bf16), held((HID + 32, HID), bf16)),
        scratch=[
            ((cells, 128), f32), ((samples // 8, 128), f32), ((HID, 16), bf16), ((HID + 16, HID), f32),
            ((HID + 16, HID), f32), ((64, HID), f32), ((16, HID), f32),
        ],
        name="backward",
    )(table, ranks, goal, shading, wide_hid, wide_misc, feats, act_one, act_two, act_three)
    even, odd, opposite = lax.optimization_barrier((even, odd, opposite))
    states = [state, sides[0], opposite, sides[1]]
    even, odd = [
        call(pair_kernel, held(own.shape, bf16), name="pair")(own, swapped(own, first))
        for own, first in ((even, True), (odd, False))
    ]

    return call(
        update_kernel,
        (
            shape((1, ENC + 1, HID)), shape((1, 2, HID, HID)), shape((1, 2, HID)), shape((1, 4, HID)),
            shape(mom_in.shape), shape(mom_hid.shape), shape(mom_bias.shape), shape(mom_out.shape),
        ),
        scratch=[((HID + 48, HID), f32), ((HID + 32, HID), f32), ((64, HID), f32)],
        name="update",
    )(
        even, swapped(even, False), odd, swapped(odd, True),
        *highs, *states, wide_misc, mom_in, mom_hid, mom_bias, mom_out,
    )


def solution(mesh):
    return jax.shard_map(
        body,
        mesh=mesh,
        in_specs=(
            P("region", None, "batch"),
            P("region", "batch"),
            P("region", "batch"),
            P("batch", None),
            P(None, "batch"),
            P("region", "batch", None),
            P("region", None, "batch", None),
            P("region", None, "batch"),
            P("region", None, "batch"),
            P(None, "region", "batch", None),
            P(None, "region", None, "batch", None),
            P(None, "region", None, "batch"),
            P(None, "region", None, "batch"),
        ),
        out_specs=(
            P("region", None, None),
            P("region", None, None, None),
            P("region", None, None),
            P("region", None, None),
            P(None, "region", "batch", None),
            P(None, "region", None, "batch", None),
            P(None, "region", None, "batch"),
            P(None, "region", None, "batch"),
        ),
        check_vma=False,
    )
```

```python
import jax
import jax.numpy as jnp
from jax import lax
from jax.experimental import pallas as pl
from jax.experimental.pallas import tpu as pltpu
from jax.sharding import PartitionSpec as P

ENC = 63
HID = 256
S = 64
N_BATCH = 4
MIB = 1 << 20
LIMIT = 32

beta_first = 0.9
beta_second = 0.95
learn_rate = 0.01
norm_eps = 1e-06
adam_eps = 1e-08

f32 = jnp.float32
bf16 = jnp.bfloat16

ROWS_IN = HID // 16
ROWS_HID = HID // N_BATCH
MISC = ROWS_IN + 2 * ROWS_HID
BLOCK = MISC + 16


def dot(left, right):
    return lax.dot_general(left, right, (((1,), (0,)), ((), ())), preferred_element_type=f32)


def dot_last(left, right):
    return lax.dot_general(left, right, (((1,), (1,)), ((), ())), preferred_element_type=f32)


def at_own_lanes(rows, own):
    source = lax.broadcasted_iota(jnp.int32, (ROWS_HID, HID), 0)
    lane = lax.broadcasted_iota(jnp.int32, (ROWS_HID, HID), 1)
    place = jnp.where(lane == source + own * ROWS_HID, 1.0, 0.0).astype(bf16)
    return dot(rows, place).astype(bf16)


def pack_weights(w_in, w_hid, b_hid, w_out, out):
    out[0:ROWS_IN, :] = w_in[0].astype(bf16)
    for layer in range(2):
        at = ROWS_IN + layer * ROWS_HID
        out[at : at + ROWS_HID, :] = w_hid[0, layer].astype(bf16)
    bias = b_hid[0]
    top = bias.astype(bf16).astype(f32)
    middle = (bias - top).astype(bf16).astype(f32)
    rest = bias - top - middle
    rows = jnp.concatenate(
        [w_out[0], top, middle, rest, jnp.zeros((6, ROWS_HID), f32)], axis=0
    ).astype(bf16)
    out[MISC:BLOCK, :] = at_own_lanes(rows, lax.axis_index("batch"))


def by_lane(rows):
    ray = lax.broadcasted_iota(jnp.int32, (128, 128), 0)
    lane = lax.broadcasted_iota(jnp.int32, (128, 128), 1)
    place = jnp.where(ray == jnp.where(lane < S, 2 * lane, 2 * (lane - S) + 1), 1.0, 0.0)
    return dot(rows.astype(bf16), place.astype(bf16))


def prepare_kernel(
    w_in, w_hid, w_out, mom_in, mom_hid, mom_bias, mom_out, spacing, counts, ranks, target,
    out, gaps, live_counts, order, goal,
):
    own = lax.axis_index("batch")

    def low(value):
        return (value - value.astype(bf16).astype(f32)).astype(bf16)

    out[0:ROWS_IN, :] = low(w_in[0])
    for layer in range(2):
        at = ROWS_IN + layer * ROWS_HID
        out[at : at + ROWS_HID, :] = low(w_hid[0, layer])
    rest = w_out[0] - w_out[0].astype(bf16).astype(f32)
    rows = jnp.concatenate([rest, jnp.zeros((12, ROWS_HID), f32)], axis=0)
    out[MISC:BLOCK, :] = at_own_lanes(rows.astype(bf16), own)
    for moment in range(2):
        base = BLOCK * (moment + 1)
        out[base : base + ROWS_IN, :] = mom_in[moment, 0].astype(bf16)
        for layer in range(2):
            at = base + ROWS_IN + layer * ROWS_HID
            out[at : at + ROWS_HID, :] = mom_hid[moment, 0, layer].astype(bf16)
        rows = jnp.concatenate(
            [mom_out[moment, 0], mom_bias[moment, 0], jnp.zeros((10, ROWS_HID), f32)], axis=0
        )
        out[base + MISC : base + BLOCK, :] = at_own_lanes(rows.astype(bf16), own)

    gaps[...] = turn(spacing[...])
    order[...] = by_lane(ranks[...].astype(f32))
    top = target[...].astype(bf16).astype(f32)
    middle = (target[...] - top).astype(bf16).astype(f32)
    rest = target[...] - top - middle
    number = counts[...].astype(f32)
    moved = by_lane(jnp.concatenate([top, middle, rest, number, jnp.zeros((6, 128), f32)], axis=0))
    goal[...] = moved[0:3] + moved[3:6] + moved[6:9]
    live_counts[...] = moved[9:10]


def turn(rows):
    turned = jnp.concatenate([rows, rows], axis=0).T
    lane = lax.broadcasted_iota(jnp.int32, (S, 2 * S), 1)
    return jnp.where(lane < S, turned[:S], turned[S:])


def running_sum(values):
    row = lax.broadcasted_iota(jnp.int32, values.shape, 0)
    step = 1
    while step < S:
        values = values + jnp.where(row >= step, pltpu.roll(values, step, 0), 0.0)
        step *= 2
    return values


def one_minus_exp(depth):
    small = depth * (1.0 - depth * (0.5 - depth * (1.0 / 6.0 - depth * (1.0 / 24.0 - depth * (1.0 / 120.0)))))
    return jnp.where(depth < 0.1, small, 1.0 - jnp.exp(-depth))


def rectified(value):
    return jnp.maximum(value.astype(bf16), jnp.zeros((), bf16))


def sigmoid(value):
    return 1.0 / (1.0 + jnp.exp(-value))


def turn_weights(wide_in, wide_hid, misc, turned_in, turned_hid, bias_cols):
    turned_in[...] = wide_in[...].astype(f32).T.astype(bf16)
    for layer in range(2):
        turned_hid[layer] = wide_hid[layer].astype(f32).T.astype(bf16)
    bias = misc[4:6] + misc[6:8] + misc[8:10]
    bias_cols[...] = jnp.concatenate([bias, jnp.zeros((6, HID), f32)], axis=0).T


def layers(samples, turned_in, turned_hid, bias_cols):
    one = rectified(dot(turned_in[...], samples))
    two = rectified(dot(turned_hid[0], one) + bias_cols[:, 0:1])
    three = rectified(dot(turned_hid[1], two) + bias_cols[:, 1:2])
    return one, two, three


def forward_kernel(
    own, from_one, from_two, from_three, feats, gaps, counts,
    wide_in, wide_hid, wide_misc, shading, summary,
    turned_in, turned_hid, bias_cols, out_rows, heads_rows,
):
    me = lax.axis_index("batch")
    misc = jnp.zeros((16, HID), f32)
    for back, block in enumerate((own, from_one, from_two, from_three)):
        owner = lax.rem(me + N_BATCH - back, N_BATCH)
        wide_in[pl.ds(pl.multiple_of(owner * ROWS_IN, 16), ROWS_IN), :] = block[0:ROWS_IN, :]
        for layer in range(2):
            at = ROWS_IN + layer * ROWS_HID
            wide_hid[layer, pl.ds(pl.multiple_of(owner * ROWS_HID, 16), ROWS_HID), :] = block[
                at : at + ROWS_HID, :
            ]
        misc = misc + block[MISC:BLOCK, :].astype(f32)
    wide_misc[...] = misc
    turn_weights(wide_in, wide_hid, misc, turned_in, turned_hid, bias_cols)
    row = lax.broadcasted_iota(jnp.int32, (16, HID), 0)
    out_rows[...] = jnp.where(row < 4, misc, 0.0).astype(bf16)

    _, _, three = layers(feats[...], turned_in, turned_hid, bias_cols)
    heads = dot(out_rows[...], three)
    for tile in range(feats.shape[1] // 128):
        heads_rows[tile * 8 : tile * 8 + 8, :] = heads[0:8, tile * 128 : (tile + 1) * 128]

    density = turn(heads_rows[pl.ds(0, S, stride=8), :])
    slot = lax.broadcasted_iota(jnp.int32, (S, 128), 0).astype(f32)
    live_gap = jnp.where(slot < counts[...], gaps[...], 0.0)
    soft = jnp.maximum(density, 0.0) + jnp.log1p(jnp.exp(-jnp.abs(density)))
    depth = soft * live_gap
    total = running_sum(depth)
    weight = jnp.exp(-(total - depth)) * one_minus_exp(depth)
    for channel in range(3):
        colour = sigmoid(turn(heads_rows[pl.ds(channel + 1, S, stride=8), :]))
        shading[channel] = colour
        summary[channel : channel + 1, :] = jnp.sum(weight * colour, axis=0, keepdims=True)
    summary[3:4, :] = -total[S - 1 : S]
    shading[3] = weight
    shading[4] = jnp.exp(-total)
    shading[5] = live_gap * sigmoid(density)


def composite(table, ranks, target, shading, reach_rows, grad_rows):
    cells = ranks.shape[0]
    order = ranks[...]
    own = lax.axis_index("region")
    prefix = jnp.zeros((cells, 128), f32)
    for cell in range(cells):
        prefix = prefix + jnp.where(
            ranks[cell : cell + 1, :] < order, table[4 * cell + 3 : 4 * cell + 4, :], 0.0
        )
    reach = jnp.exp(prefix)
    reach_rows[...] = reach
    own_reach = reach_rows[pl.ds(own, 1), :]
    later = order > ranks[pl.ds(own, 1), :]
    grad_seg = []
    grad_log = jnp.zeros((1, 128), f32)
    for channel in range(3):
        lit = reach * table[pl.ds(channel, cells, stride=4), :]
        grad_colour = 2.0 * (jnp.sum(lit, axis=0, keepdims=True) - target[channel : channel + 1, :])
        behind = jnp.sum(jnp.where(later, lit, 0.0), axis=0, keepdims=True)
        grad_log = grad_log + grad_colour * behind
        grad_seg.append(own_reach * grad_colour)
    weight = shading[3]
    emit = grad_seg[0] * shading[0] + grad_seg[1] * shading[1] + grad_seg[2] * shading[2]
    carried = emit * weight
    running = running_sum(carried)
    after = running[S - 1 : S] - running
    grad_depth = emit * shading[4] - after - grad_log
    grad_rows[...] = jnp.zeros(grad_rows.shape, f32)
    grad_rows[pl.ds(0, S, stride=16), :] = turn(grad_depth * shading[5])
    for channel in range(3):
        colour = shading[channel]
        shade = grad_seg[channel] * weight * colour * (1.0 - colour)
        grad_rows[pl.ds(channel + 1, S, stride=16), :] = turn(shade)


def masked(act, back):
    return jnp.where(act > 0, back.astype(bf16), jnp.zeros((), bf16))


def backward_kernel(
    table, ranks, target, shading, wide_in, wide_hid, wide_misc, feats,
    even, odd,
    reach_rows, grad_rows, out_cols, turned_in, turned_hid, bias_cols, act_one, act_two, act_three,
):
    turn_weights(wide_in, wide_hid, wide_misc[...], turned_in, turned_hid, bias_cols)
    composite(table, ranks, target, shading, reach_rows, grad_rows)
    row = lax.broadcasted_iota(jnp.int32, (16, HID), 0)
    out_cols[...] = jnp.where(row < 4, wide_misc[...], 0.0).T.astype(bf16)
    samples = feats[...]
    act_one[...], act_two[...], act_three[...] = layers(samples, turned_in, turned_hid, bias_cols)
    one, two, three = act_one[...], act_two[...], act_three[...]
    heads = jnp.concatenate(
        [grad_rows[tile * 16 : tile * 16 + 16, :] for tile in range(feats.shape[1] // 128)], axis=1
    ).astype(bf16)
    ones = jnp.ones((16, feats.shape[1]), bf16)
    back_three = masked(three, dot(out_cols[...], heads))
    sum_out = dot_last(heads, three)
    back_two = masked(two, dot(wide_hid[1], back_three))
    sum_third = dot_last(jnp.concatenate([two, ones], axis=0), back_three)
    back_one = masked(one, dot(wide_hid[0], back_two))
    sum_second = dot_last(jnp.concatenate([one, ones], axis=0), back_two)
    sum_first = dot_last(samples, back_one)

    misc = jnp.where(row < 4, sum_out, 0.0)
    misc = misc + jnp.where(row == 4, sum_second[HID : HID + 16, :], 0.0)
    misc = misc + jnp.where(row == 5, sum_third[HID : HID + 16, :], 0.0)
    even[0:HID, :] = sum_third[0:HID, :].astype(bf16)
    even[HID : HID + 32, :] = sum_first[0:32, :].astype(bf16)
    even[HID + 32 : HID + 48, :] = misc.astype(bf16)
    odd[0:HID, :] = sum_second[0:HID, :].astype(bf16)
    odd[HID : HID + 32, :] = sum_first[32:64, :].astype(bf16)


def pair_kernel(own, other, total):
    total[...] = (own[...].astype(f32) + other[...].astype(f32)).astype(bf16)


def adam(grad, first, second, scale):
    scaled = grad * scale
    first = beta_first * first + (1.0 - beta_first) * scaled
    second = beta_second * second + (1.0 - beta_second) * scaled * scaled
    return first, second, learn_rate * first / (jnp.sqrt(second) + adam_eps)


def update_kernel(
    even, even_other, odd, odd_other,
    high_0, high_1, high_2, high_3,
    state_0, state_1, state_2, state_3,
    wide_misc, mom_in, mom_hid, mom_bias, mom_out,
    new_in, new_hid, new_bias, new_out,
    out_in, out_hid, out_bias, out_out,
    upper, lower, first_rows,
):
    me = lax.axis_index("batch")
    param_count = (ENC + 1) * HID + 2 * HID * HID + 6 * HID
    upper[...] = even[...].astype(f32) + even_other[...].astype(f32)
    lower[...] = odd[...].astype(f32) + odd_other[...].astype(f32)
    first_rows[0:32, :] = upper[HID : HID + 32, :]
    first_rows[32:64, :] = lower[HID : HID + 32, :]
    grad_misc = upper[HID + 32 : HID + 48, :]
    squares = jnp.sum(upper[...] * upper[...], axis=0, keepdims=True) + jnp.sum(
        lower[...] * lower[...], axis=0, keepdims=True
    )
    total = jnp.sum(squares, axis=1, keepdims=True)
    scale = lax.rsqrt(total / param_count + norm_eps)

    def fresh(grad, high, state, at, rows):
        _, _, change = adam(
            grad,
            state[BLOCK + at : BLOCK + at + rows, :].astype(f32),
            state[2 * BLOCK + at : 2 * BLOCK + at + rows, :].astype(f32),
            scale,
        )
        value = high[at : at + rows, :].astype(f32) + state[at : at + rows, :].astype(f32)
        return value - change

    highs = (high_0, high_1, high_2, high_3)
    states = (state_0, state_1, state_2, state_3)
    low_misc = jnp.zeros((16, HID), f32)
    first_misc = jnp.zeros((16, HID), f32)
    second_misc = jnp.zeros((16, HID), f32)
    for back in range(N_BATCH):
        owner = lax.rem(me + N_BATCH - back, N_BATCH)
        high, state = highs[back], states[back]
        hid = pl.ds(pl.multiple_of(owner * ROWS_HID, 16), ROWS_HID)
        new_hid[0, 0, hid, :] = fresh(lower[hid, :], high, state, ROWS_IN, ROWS_HID)
        new_hid[0, 1, hid, :] = fresh(upper[hid, :], high, state, ROWS_IN + ROWS_HID, ROWS_HID)
        first = pl.ds(pl.multiple_of(owner * ROWS_IN, 16), ROWS_IN)
        grad = first_rows[first, :]
        new_in[0, first, :] = fresh(grad, high, state, 0, ROWS_IN)
        low_misc = low_misc + state[MISC:BLOCK, :].astype(f32)
        first_misc = first_misc + state[BLOCK + MISC : 2 * BLOCK, :].astype(f32)
        second_misc = second_misc + state[2 * BLOCK + MISC : 3 * BLOCK, :].astype(f32)

    _, _, change = adam(grad_misc, first_misc, second_misc, scale)
    weights = wide_misc[...]
    new_out[0] = weights[0:4] + low_misc[0:4] - change[0:4]
    new_bias[0] = weights[4:6] + weights[6:8] + weights[8:10] - change[4:6]

    own = pl.ds(pl.multiple_of(me * ROWS_HID, 16), ROWS_HID)
    for layer, grads in ((0, lower), (1, upper)):
        moments = adam(grads[own, :], mom_hid[0, 0, layer], mom_hid[1, 0, layer], scale)
        out_hid[0, 0, layer] = moments[0]
        out_hid[1, 0, layer] = moments[1]
    grad = first_rows[pl.ds(pl.multiple_of(me * ROWS_IN, 16), ROWS_IN), :]
    moments = adam(grad, mom_in[0, 0], mom_in[1, 0], scale)
    out_in[0, 0] = moments[0]
    out_in[1, 0] = moments[1]
    own_misc = jnp.zeros((16, ROWS_HID), f32)
    for owner in range(N_BATCH):
        part = grad_misc[:, owner * ROWS_HID : (owner + 1) * ROWS_HID]
        own_misc = own_misc + jnp.where(me == owner, part, 0.0)
    moments = adam(own_misc[0:4], mom_out[0, 0], mom_out[1, 0], scale)
    out_out[0, 0] = moments[0]
    out_out[1, 0] = moments[1]
    moments = adam(own_misc[4:6], mom_bias[0, 0], mom_bias[1, 0], scale)
    out_bias[0, 0] = moments[0]
    out_bias[1, 0] = moments[1]


def fetched(kernel, fetch, outs):
    def run(*refs):
        sources, rest = refs[:fetch], refs[fetch : fetch + outs]
        copies, sem = refs[fetch + outs : -1], refs[-1]
        moves = [pltpu.make_async_copy(a, b, sem.at[i]) for i, (a, b) in enumerate(zip(sources, copies))]
        for move in moves:
            move.start()
        for move in moves:
            move.wait()
        kernel(*copies, *rest)

    return run


def call_on_hbm(kernel, outs, name, *arrays):
    outs = outs if isinstance(outs, tuple) else (outs,)
    return pl.pallas_call(
        fetched(kernel, len(arrays), len(outs)),
        out_shape=outs,
        in_specs=[pl.BlockSpec(memory_space=pltpu.HBM)] * len(arrays),
        scratch_shapes=[pltpu.VMEM(a.shape, a.dtype) for a in arrays]
        + [pltpu.SemaphoreType.DMA((len(arrays),))],
        compiler_params=pltpu.CompilerParams(vmem_limit_bytes=60 * MIB),
        name=name,
    )(*arrays)


def call(kernel, outs, scratch=(), name=None):
    return pl.pallas_call(
        kernel,
        out_shape=outs,
        scratch_shapes=[pltpu.VMEM(*s) for s in scratch],
        compiler_params=pltpu.CompilerParams(vmem_limit_bytes=LIMIT * MIB),
        name=name,
    )


def from_others(block):
    return [
        lax.ppermute(block, "batch", [(i, (i + hop) % N_BATCH) for i in range(N_BATCH)])
        for hop in (1, 2, 3)
    ]


def swapped(block, first):
    pairs = [(0, 1), (2, 3)] if first else [(1, 2), (3, 0)]
    return lax.ppermute(block, "batch", pairs + [(j, i) for i, j in pairs])


def held(dims, dtype=f32):
    return pltpu.VMEM(dims, dtype)


def shape(dims, dtype=f32):
    return jax.ShapeDtypeStruct(dims, dtype)


def body(
    features, spacing, counts, depth_rank, target,
    w_in, w_hid, b_hid, w_out,
    mom_in, mom_hid, mom_bias, mom_out,
):
    samples = features.shape[2]
    rays = samples // S
    cells = depth_rank.shape[1]

    (block,) = call_on_hbm(
        pack_weights, held((BLOCK, HID), bf16), "pack_weights", w_in, w_hid, b_hid, w_out
    )
    block, spacing = lax.optimization_barrier((block, spacing))
    highs = [block] + from_others(block)
    state, gaps, live_counts, ranks, goal = call_on_hbm(
        prepare_kernel,
        (
            held((3 * BLOCK, HID), bf16), held((S, rays)), held((1, rays)), held((cells, rays)),
            held((3, rays)),
        ),
        "prepare",
        w_in, w_hid, w_out, mom_in, mom_hid, mom_bias, mom_out,
        spacing.reshape(rays // 2, 2 * S), counts, depth_rank.T, target,
    )
    feats = jnp.concatenate([features[0], jnp.ones((1, samples), bf16)], axis=0)
    state, feats, *highs[1:] = lax.optimization_barrier((state, feats, *highs[1:]))
    states = [state] + from_others(state)

    turned = [((HID, ENC + 1), bf16), ((2, HID, HID), bf16), ((HID, 8), f32)]
    wide_in, wide_hid, wide_misc, shading, summary = call(
        forward_kernel,
        (
            held((ENC + 1, HID), bf16), held((2, HID, HID), bf16), held((16, HID)), held((6, S, 128)),
            held((4, rays)),
        ),
        scratch=turned + [((16, HID), bf16), ((samples // 16, 128), f32)],
        name="forward",
    )(*highs, feats, gaps, live_counts)

    table = lax.all_to_all(
        jnp.broadcast_to(summary[None], (cells, 4, rays)), "region", 0, 0, tiled=True
    ).reshape(cells * 4, rays)

    even, odd = call(
        backward_kernel,
        (held((HID + 48, HID), bf16), held((HID + 32, HID), bf16)),
        scratch=[((cells, 128), f32), ((samples // 8, 128), f32), ((HID, 16), bf16)]
        + turned
        + [((HID, samples), bf16)] * 3,
        name="backward",
    )(table, ranks, goal, shading, wide_in, wide_hid, wide_misc, feats)
    even, odd, *states = lax.optimization_barrier((even, odd, *states))
    even, odd = [
        call(pair_kernel, held(own.shape, bf16), name="pair")(own, swapped(own, first))
        for own, first in ((even, True), (odd, False))
    ]

    return call(
        update_kernel,
        (
            shape((1, ENC + 1, HID)), shape((1, 2, HID, HID)), shape((1, 2, HID)), shape((1, 4, HID)),
            shape(mom_in.shape), shape(mom_hid.shape), shape(mom_bias.shape), shape(mom_out.shape),
        ),
        scratch=[((HID + 48, HID), f32), ((HID + 32, HID), f32), ((64, HID), f32)],
        name="update",
    )(
        even, swapped(even, False), odd, swapped(odd, True),
        *highs, *states, wide_misc, mom_in, mom_hid, mom_bias, mom_out,
    )


def solution(mesh):
    return jax.shard_map(
        body,
        mesh=mesh,
        in_specs=(
            P("region", None, "batch"),
            P("region", "batch"),
            P("region", "batch"),
            P("batch", None),
            P(None, "batch"),
            P("region", "batch", None),
            P("region", None, "batch", None),
            P("region", None, "batch"),
            P("region", None, "batch"),
            P(None, "region", "batch", None),
            P(None, "region", None, "batch", None),
            P(None, "region", None, "batch"),
            P(None, "region", None, "batch"),
        ),
        out_specs=(
            P("region", None, None),
            P("region", None, None, None),
            P("region", None, None),
            P("region", None, None),
            P(None, "region", "batch", None),
            P(None, "region", None, "batch", None),
            P(None, "region", None, "batch"),
            P(None, "region", None, "batch"),
        ),
        check_vma=False,
    )
```

```python
import jax
import jax.numpy as jnp
from jax import lax
from jax.experimental import pallas as pl
from jax.experimental.pallas import tpu as pltpu
from jax.sharding import PartitionSpec as P

ENC = 63
HID = 256
S = 64
N_BATCH = 4
MIB = 1 << 20
LIMIT = 32

beta_first = 0.9
beta_second = 0.95
learn_rate = 0.01
norm_eps = 1e-06
adam_eps = 1e-08

f32 = jnp.float32
bf16 = jnp.bfloat16

ROWS_IN = HID // 16
ROWS_HID = HID // N_BATCH
MISC = ROWS_IN + 2 * ROWS_HID
BLOCK = MISC + 16


def dot(left, right):
    return lax.dot_general(left, right, (((1,), (0,)), ((), ())), preferred_element_type=f32)


def dot_last(left, right):
    return lax.dot_general(left, right, (((1,), (1,)), ((), ())), preferred_element_type=f32)


def at_own_lanes(rows, own):
    source = lax.broadcasted_iota(jnp.int32, (ROWS_HID, HID), 0)
    lane = lax.broadcasted_iota(jnp.int32, (ROWS_HID, HID), 1)
    place = jnp.where(lane == source + own * ROWS_HID, 1.0, 0.0).astype(bf16)
    return dot(rows, place).astype(bf16)


def pack_weights(w_in, w_hid, b_hid, w_out, out):
    out[0:ROWS_IN, :] = w_in[0].astype(bf16)
    for layer in range(2):
        at = ROWS_IN + layer * ROWS_HID
        out[at : at + ROWS_HID, :] = w_hid[0, layer].astype(bf16)
    bias = b_hid[0]
    top = bias.astype(bf16).astype(f32)
    middle = (bias - top).astype(bf16).astype(f32)
    rest = bias - top - middle
    rows = jnp.concatenate(
        [w_out[0], top, middle, rest, jnp.zeros((6, ROWS_HID), f32)], axis=0
    ).astype(bf16)
    out[MISC:BLOCK, :] = at_own_lanes(rows, lax.axis_index("batch"))


def by_lane(rows):
    ray = lax.broadcasted_iota(jnp.int32, (128, 128), 0)
    lane = lax.broadcasted_iota(jnp.int32, (128, 128), 1)
    place = jnp.where(ray == jnp.where(lane < S, 2 * lane, 2 * (lane - S) + 1), 1.0, 0.0)
    return dot(rows.astype(bf16), place.astype(bf16))


def prepare_kernel(
    w_in, w_hid, w_out, mom_in, mom_hid, mom_bias, mom_out, spacing, counts, ranks, target,
    out, gaps, live_counts, order, goal,
):
    own = lax.axis_index("batch")

    def low(value):
        return (value - value.astype(bf16).astype(f32)).astype(bf16)

    out[0:ROWS_IN, :] = low(w_in[0])
    for layer in range(2):
        at = ROWS_IN + layer * ROWS_HID
        out[at : at + ROWS_HID, :] = low(w_hid[0, layer])
    rest = w_out[0] - w_out[0].astype(bf16).astype(f32)
    rows = jnp.concatenate([rest, jnp.zeros((12, ROWS_HID), f32)], axis=0)
    out[MISC:BLOCK, :] = at_own_lanes(rows.astype(bf16), own)
    for moment in range(2):
        base = BLOCK * (moment + 1)
        out[base : base + ROWS_IN, :] = mom_in[moment, 0].astype(bf16)
        for layer in range(2):
            at = base + ROWS_IN + layer * ROWS_HID
            out[at : at + ROWS_HID, :] = mom_hid[moment, 0, layer].astype(bf16)
        rows = jnp.concatenate(
            [mom_out[moment, 0], mom_bias[moment, 0], jnp.zeros((10, ROWS_HID), f32)], axis=0
        )
        out[base + MISC : base + BLOCK, :] = at_own_lanes(rows.astype(bf16), own)

    gaps[...] = turn(spacing[...])
    order[...] = by_lane(ranks[...].astype(f32))
    top = target[...].astype(bf16).astype(f32)
    middle = (target[...] - top).astype(bf16).astype(f32)
    rest = target[...] - top - middle
    number = counts[...].astype(f32)
    moved = by_lane(jnp.concatenate([top, middle, rest, number, jnp.zeros((6, 128), f32)], axis=0))
    goal[...] = moved[0:3] + moved[3:6] + moved[6:9]
    live_counts[...] = moved[9:10]


def turn(rows):
    turned = jnp.concatenate([rows, rows], axis=0).T
    lane = lax.broadcasted_iota(jnp.int32, (S, 2 * S), 1)
    return jnp.where(lane < S, turned[:S], turned[S:])


def running_sum(values):
    row = lax.broadcasted_iota(jnp.int32, values.shape, 0)
    step = 1
    while step < S:
        values = values + jnp.where(row >= step, pltpu.roll(values, step, 0), 0.0)
        step *= 2
    return values


def one_minus_exp(depth):
    small = depth * (1.0 - depth * (0.5 - depth * (1.0 / 6.0 - depth * (1.0 / 24.0 - depth * (1.0 / 120.0)))))
    return jnp.where(depth < 0.1, small, 1.0 - jnp.exp(-depth))


def rectified(value):
    return jnp.maximum(value.astype(bf16), jnp.zeros((), bf16))


def sigmoid(value):
    return 1.0 / (1.0 + jnp.exp(-value))


def turn_weights(wide_in, wide_hid, misc, turned_in, turned_hid, bias_cols):
    turned_in[...] = wide_in[...].astype(f32).T.astype(bf16)
    for layer in range(2):
        turned_hid[layer] = wide_hid[layer].astype(f32).T.astype(bf16)
    bias = misc[4:6] + misc[6:8] + misc[8:10]
    bias_cols[...] = jnp.concatenate([bias, jnp.zeros((6, HID), f32)], axis=0).T


def layers(samples, turned_in, turned_hid, bias_cols):
    one = rectified(dot(turned_in[...], samples))
    two = rectified(dot(turned_hid[0], one) + bias_cols[:, 0:1])
    three = rectified(dot(turned_hid[1], two) + bias_cols[:, 1:2])
    return one, two, three


def forward_kernel(
    own, from_one, from_two, from_three, feats, gaps, counts,
    wide_in, wide_hid, wide_misc, shading, sent,
    turned_in, turned_hid, bias_cols, out_rows, heads_rows, summary,
):
    me = lax.axis_index("batch")
    misc = jnp.zeros((16, HID), f32)
    for back, block in enumerate((own, from_one, from_two, from_three)):
        owner = lax.rem(me + N_BATCH - back, N_BATCH)
        wide_in[pl.ds(pl.multiple_of(owner * ROWS_IN, 16), ROWS_IN), :] = block[0:ROWS_IN, :]
        for layer in range(2):
            at = ROWS_IN + layer * ROWS_HID
            wide_hid[layer, pl.ds(pl.multiple_of(owner * ROWS_HID, 16), ROWS_HID), :] = block[
                at : at + ROWS_HID, :
            ]
        misc = misc + block[MISC:BLOCK, :].astype(f32)
    wide_misc[...] = misc
    turn_weights(wide_in, wide_hid, misc, turned_in, turned_hid, bias_cols)
    row = lax.broadcasted_iota(jnp.int32, (16, HID), 0)
    out_rows[...] = jnp.where(row < 4, misc, 0.0).astype(bf16)

    _, _, three = layers(feats[...], turned_in, turned_hid, bias_cols)
    heads = dot(out_rows[...], three)
    for tile in range(feats.shape[1] // 128):
        heads_rows[tile * 8 : tile * 8 + 8, :] = heads[0:8, tile * 128 : (tile + 1) * 128]

    density = turn(heads_rows[pl.ds(0, S, stride=8), :])
    slot = lax.broadcasted_iota(jnp.int32, (S, 128), 0).astype(f32)
    live_gap = jnp.where(slot < counts[...], gaps[...], 0.0)
    soft = jnp.maximum(density, 0.0) + jnp.log1p(jnp.exp(-jnp.abs(density)))
    depth = soft * live_gap
    total = running_sum(depth)
    weight = jnp.exp(-(total - depth)) * one_minus_exp(depth)
    for channel in range(3):
        colour = sigmoid(turn(heads_rows[pl.ds(channel + 1, S, stride=8), :]))
        shading[channel] = colour
        summary[channel : channel + 1, :] = jnp.sum(weight * colour, axis=0, keepdims=True)
    summary[3:4, :] = -total[S - 1 : S]
    shading[3] = weight
    shading[4] = jnp.exp(-total)
    shading[5] = live_gap * sigmoid(density)
    for cell in range(sent.shape[0]):
        sent[cell] = summary[...]


def composite(table, ranks, target, shading, reach_rows, grad_rows):
    cells = ranks.shape[0]
    order = ranks[...]
    own = lax.axis_index("region")
    prefix = jnp.zeros((cells, 128), f32)
    for cell in range(cells):
        prefix = prefix + jnp.where(
            ranks[cell : cell + 1, :] < order, table[4 * cell + 3 : 4 * cell + 4, :], 0.0
        )
    reach = jnp.exp(prefix)
    reach_rows[...] = reach
    own_reach = reach_rows[pl.ds(own, 1), :]
    later = order > ranks[pl.ds(own, 1), :]
    grad_seg = []
    grad_log = jnp.zeros((1, 128), f32)
    for channel in range(3):
        lit = reach * table[pl.ds(channel, cells, stride=4), :]
        grad_colour = 2.0 * (jnp.sum(lit, axis=0, keepdims=True) - target[channel : channel + 1, :])
        behind = jnp.sum(jnp.where(later, lit, 0.0), axis=0, keepdims=True)
        grad_log = grad_log + grad_colour * behind
        grad_seg.append(own_reach * grad_colour)
    weight = shading[3]
    emit = grad_seg[0] * shading[0] + grad_seg[1] * shading[1] + grad_seg[2] * shading[2]
    carried = emit * weight
    running = running_sum(carried)
    after = running[S - 1 : S] - running
    grad_depth = emit * shading[4] - after - grad_log
    grad_rows[...] = jnp.zeros(grad_rows.shape, f32)
    grad_rows[pl.ds(0, S, stride=16), :] = turn(grad_depth * shading[5])
    for channel in range(3):
        colour = shading[channel]
        shade = grad_seg[channel] * weight * colour * (1.0 - colour)
        grad_rows[pl.ds(channel + 1, S, stride=16), :] = turn(shade)


def masked(act, back):
    return jnp.where(act > 0, back.astype(bf16), jnp.zeros((), bf16))


def backward_kernel(
    table, ranks, target, shading, wide_in, wide_hid, wide_misc, feats,
    even, odd,
    reach_rows, grad_rows, out_cols, turned_in, turned_hid, bias_cols, act_one, act_two, act_three,
):
    turn_weights(wide_in, wide_hid, wide_misc[...], turned_in, turned_hid, bias_cols)
    composite(table, ranks, target, shading, reach_rows, grad_rows)
    row = lax.broadcasted_iota(jnp.int32, (16, HID), 0)
    out_cols[...] = jnp.where(row < 4, wide_misc[...], 0.0).T.astype(bf16)
    samples = feats[...]
    act_one[...], act_two[...], act_three[...] = layers(samples, turned_in, turned_hid, bias_cols)
    one, two, three = act_one[...], act_two[...], act_three[...]
    heads = jnp.concatenate(
        [grad_rows[tile * 16 : tile * 16 + 16, :] for tile in range(feats.shape[1] // 128)], axis=1
    ).astype(bf16)
    ones = jnp.ones((16, feats.shape[1]), bf16)
    back_three = masked(three, dot(out_cols[...], heads))
    sum_out = dot_last(heads, three)
    back_two = masked(two, dot(wide_hid[1], back_three))
    sum_third = dot_last(jnp.concatenate([two, ones], axis=0), back_three)
    back_one = masked(one, dot(wide_hid[0], back_two))
    sum_second = dot_last(jnp.concatenate([one, ones], axis=0), back_two)
    sum_first = dot_last(samples, back_one)

    misc = jnp.where(row < 4, sum_out, 0.0)
    misc = misc + jnp.where(row == 4, sum_second[HID : HID + 16, :], 0.0)
    misc = misc + jnp.where(row == 5, sum_third[HID : HID + 16, :], 0.0)
    even[0:HID, :] = sum_third[0:HID, :].astype(bf16)
    even[HID : HID + 32, :] = sum_first[0:32, :].astype(bf16)
    even[HID + 32 : HID + 48, :] = misc.astype(bf16)
    odd[0:HID, :] = sum_second[0:HID, :].astype(bf16)
    odd[HID : HID + 32, :] = sum_first[32:64, :].astype(bf16)


def pair_kernel(own, other, total):
    total[...] = (own[...].astype(f32) + other[...].astype(f32)).astype(bf16)


def adam(grad, first, second, scale):
    scaled = grad * scale
    first = beta_first * first + (1.0 - beta_first) * scaled
    second = beta_second * second + (1.0 - beta_second) * scaled * scaled
    return first, second, learn_rate * first / (jnp.sqrt(second) + adam_eps)


def update_kernel(
    even, even_other, odd, odd_other,
    high_0, high_1, high_2, high_3,
    state_0, state_1, state_2, state_3,
    wide_misc, mom_in, mom_hid, mom_bias, mom_out,
    new_in, new_hid, new_bias, new_out,
    out_in, out_hid, out_bias, out_out,
    upper, lower, first_rows,
):
    me = lax.axis_index("batch")
    param_count = (ENC + 1) * HID + 2 * HID * HID + 6 * HID
    upper[...] = even[...].astype(f32) + even_other[...].astype(f32)
    lower[...] = odd[...].astype(f32) + odd_other[...].astype(f32)
    first_rows[0:32, :] = upper[HID : HID + 32, :]
    first_rows[32:64, :] = lower[HID : HID + 32, :]
    grad_misc = upper[HID + 32 : HID + 48, :]
    squares = jnp.sum(upper[...] * upper[...], axis=0, keepdims=True) + jnp.sum(
        lower[...] * lower[...], axis=0, keepdims=True
    )
    total = jnp.sum(squares, axis=1, keepdims=True)
    scale = lax.rsqrt(total / param_count + norm_eps)

    def fresh(grad, high, state, at, rows):
        _, _, change = adam(
            grad,
            state[BLOCK + at : BLOCK + at + rows, :].astype(f32),
            state[2 * BLOCK + at : 2 * BLOCK + at + rows, :].astype(f32),
            scale,
        )
        value = high[at : at + rows, :].astype(f32) + state[at : at + rows, :].astype(f32)
        return value - change

    highs = (high_0, high_1, high_2, high_3)
    states = (state_0, state_1, state_2, state_3)
    low_misc = jnp.zeros((16, HID), f32)
    first_misc = jnp.zeros((16, HID), f32)
    second_misc = jnp.zeros((16, HID), f32)
    for back in range(N_BATCH):
        owner = lax.rem(me + N_BATCH - back, N_BATCH)
        high, state = highs[back], states[back]
        hid = pl.ds(pl.multiple_of(owner * ROWS_HID, 16), ROWS_HID)
        new_hid[0, 0, hid, :] = fresh(lower[hid, :], high, state, ROWS_IN, ROWS_HID)
        new_hid[0, 1, hid, :] = fresh(upper[hid, :], high, state, ROWS_IN + ROWS_HID, ROWS_HID)
        first = pl.ds(pl.multiple_of(owner * ROWS_IN, 16), ROWS_IN)
        grad = first_rows[first, :]
        new_in[0, first, :] = fresh(grad, high, state, 0, ROWS_IN)
        low_misc = low_misc + state[MISC:BLOCK, :].astype(f32)
        first_misc = first_misc + state[BLOCK + MISC : 2 * BLOCK, :].astype(f32)
        second_misc = second_misc + state[2 * BLOCK + MISC : 3 * BLOCK, :].astype(f32)

    _, _, change = adam(grad_misc, first_misc, second_misc, scale)
    weights = wide_misc[...]
    new_out[0] = weights[0:4] + low_misc[0:4] - change[0:4]
    new_bias[0] = weights[4:6] + weights[6:8] + weights[8:10] - change[4:6]

    own = pl.ds(pl.multiple_of(me * ROWS_HID, 16), ROWS_HID)
    for layer, grads in ((0, lower), (1, upper)):
        moments = adam(grads[own, :], mom_hid[0, 0, layer], mom_hid[1, 0, layer], scale)
        out_hid[0, 0, layer] = moments[0]
        out_hid[1, 0, layer] = moments[1]
    grad = first_rows[pl.ds(pl.multiple_of(me * ROWS_IN, 16), ROWS_IN), :]
    moments = adam(grad, mom_in[0, 0], mom_in[1, 0], scale)
    out_in[0, 0] = moments[0]
    out_in[1, 0] = moments[1]
    own_misc = jnp.zeros((16, ROWS_HID), f32)
    for owner in range(N_BATCH):
        part = grad_misc[:, owner * ROWS_HID : (owner + 1) * ROWS_HID]
        own_misc = own_misc + jnp.where(me == owner, part, 0.0)
    moments = adam(own_misc[0:4], mom_out[0, 0], mom_out[1, 0], scale)
    out_out[0, 0] = moments[0]
    out_out[1, 0] = moments[1]
    moments = adam(own_misc[4:6], mom_bias[0, 0], mom_bias[1, 0], scale)
    out_bias[0, 0] = moments[0]
    out_bias[1, 0] = moments[1]


def fetched(kernel, fetch, outs):
    def run(*refs):
        sources, rest = refs[:fetch], refs[fetch : fetch + outs]
        copies, sem = refs[fetch + outs : -1], refs[-1]
        moves = [pltpu.make_async_copy(a, b, sem.at[i]) for i, (a, b) in enumerate(zip(sources, copies))]
        for move in moves:
            move.start()
        for move in moves:
            move.wait()
        kernel(*copies, *rest)

    return run


def call_on_hbm(kernel, outs, name, *arrays):
    outs = outs if isinstance(outs, tuple) else (outs,)
    return pl.pallas_call(
        fetched(kernel, len(arrays), len(outs)),
        out_shape=outs,
        in_specs=[pl.BlockSpec(memory_space=pltpu.HBM)] * len(arrays),
        scratch_shapes=[pltpu.VMEM(a.shape, a.dtype) for a in arrays]
        + [pltpu.SemaphoreType.DMA((len(arrays),))],
        compiler_params=pltpu.CompilerParams(vmem_limit_bytes=60 * MIB),
        name=name,
    )(*arrays)


def call(kernel, outs, scratch=(), name=None):
    return pl.pallas_call(
        kernel,
        out_shape=outs,
        scratch_shapes=[pltpu.VMEM(*s) for s in scratch],
        compiler_params=pltpu.CompilerParams(vmem_limit_bytes=LIMIT * MIB),
        name=name,
    )


def from_others(block):
    return [
        lax.ppermute(block, "batch", [(i, (i + hop) % N_BATCH) for i in range(N_BATCH)])
        for hop in (1, 2, 3)
    ]


def swapped(block, first):
    pairs = [(0, 1), (2, 3)] if first else [(1, 2), (3, 0)]
    return lax.ppermute(block, "batch", pairs + [(j, i) for i, j in pairs])


def held(dims, dtype=f32):
    return pltpu.VMEM(dims, dtype)


def shape(dims, dtype=f32):
    return jax.ShapeDtypeStruct(dims, dtype)


def body(
    features, spacing, counts, depth_rank, target,
    w_in, w_hid, b_hid, w_out,
    mom_in, mom_hid, mom_bias, mom_out,
):
    samples = features.shape[2]
    rays = samples // S
    cells = depth_rank.shape[1]

    (block,) = call_on_hbm(
        pack_weights, held((BLOCK, HID), bf16), "pack_weights", w_in, w_hid, b_hid, w_out
    )
    block, spacing = lax.optimization_barrier((block, spacing))
    highs = [block] + from_others(block)
    state, gaps, live_counts, ranks, goal = call_on_hbm(
        prepare_kernel,
        (
            held((3 * BLOCK, HID), bf16), held((S, rays)), held((1, rays)), held((cells, rays)),
            held((3, rays)),
        ),
        "prepare",
        w_in, w_hid, w_out, mom_in, mom_hid, mom_bias, mom_out,
        spacing.reshape(rays // 2, 2 * S), counts, depth_rank.T, target,
    )
    feats = jnp.concatenate([features[0], jnp.ones((1, samples), bf16)], axis=0)
    state, feats, *highs[1:] = lax.optimization_barrier((state, feats, *highs[1:]))
    states = [state] + from_others(state)

    turned = [((HID, ENC + 1), bf16), ((2, HID, HID), bf16), ((HID, 8), f32)]
    wide_in, wide_hid, wide_misc, shading, sent = call(
        forward_kernel,
        (
            held((ENC + 1, HID), bf16), held((2, HID, HID), bf16), held((16, HID)), held((6, S, 128)),
            shape((cells, 4, rays)),
        ),
        scratch=turned + [((16, HID), bf16), ((samples // 16, 128), f32), ((4, rays), f32)],
        name="forward",
    )(*highs, feats, gaps, live_counts)

    table = lax.all_to_all(sent, "region", 0, 0, tiled=True).reshape(cells * 4, rays)

    even, odd = call(
        backward_kernel,
        (held((HID + 48, HID), bf16), held((HID + 32, HID), bf16)),
        scratch=[((cells, 128), f32), ((samples // 8, 128), f32), ((HID, 16), bf16)]
        + turned
        + [((HID, samples), bf16)] * 3,
        name="backward",
    )(table, ranks, goal, shading, wide_in, wide_hid, wide_misc, feats)
    even, odd, *states = lax.optimization_barrier((even, odd, *states))
    even, odd = [
        call(pair_kernel, held(own.shape, bf16), name="pair")(own, swapped(own, first))
        for own, first in ((even, True), (odd, False))
    ]

    return call(
        update_kernel,
        (
            shape((1, ENC + 1, HID)), shape((1, 2, HID, HID)), shape((1, 2, HID)), shape((1, 4, HID)),
            shape(mom_in.shape), shape(mom_hid.shape), shape(mom_bias.shape), shape(mom_out.shape),
        ),
        scratch=[((HID + 48, HID), f32), ((HID + 32, HID), f32), ((64, HID), f32)],
        name="update",
    )(
        even, swapped(even, False), odd, swapped(odd, True),
        *highs, *states, wide_misc, mom_in, mom_hid, mom_bias, mom_out,
    )


def solution(mesh):
    return jax.shard_map(
        body,
        mesh=mesh,
        in_specs=(
            P("region", None, "batch"),
            P("region", "batch"),
            P("region", "batch"),
            P("batch", None),
            P(None, "batch"),
            P("region", "batch", None),
            P("region", None, "batch", None),
            P("region", None, "batch"),
            P("region", None, "batch"),
            P(None, "region", "batch", None),
            P(None, "region", None, "batch", None),
            P(None, "region", None, "batch"),
            P(None, "region", None, "batch"),
        ),
        out_specs=(
            P("region", None, None),
            P("region", None, None, None),
            P("region", None, None),
            P("region", None, None),
            P(None, "region", "batch", None),
            P(None, "region", None, "batch", None),
            P(None, "region", None, "batch"),
            P(None, "region", None, "batch"),
        ),
        check_vma=False,
    )
```
